32 devices in a mesh: lon: 8 (over z, core), lat: 4 (over y, x).
Axes of the slice: x: 2, y: 2, z: 4, core: 2. Of those that a mesh axis runs over, the one named last changes fastest.
Arguments:
- perturbations: float32 [12, 3, 64, 1024], P(None, None, 'lat', 'lon'), as said below
- base_wind: float32 [2, 64, 1024], P(None, 'lat', 'lon'), may hold values from -4 to 4
- base_height: float32 [64, 1024], P('lat', 'lon'), may hold values from 0.5 to 1.5
Outputs:
- fields: float32 [12, 3, 64, 1024], P(None, None, 'lat', 'lon')
- factor: float32 [12, 12], replicated
The draws below stay inside these ranges and needn't reach their ends.
Inputs may be any that keep to these rules, and one draw needn't show every extreme that they name: `perturbations`: finite real values.
All inputs are finite; a program needn't handle non-finite values.
Results may differ from the reference program's by a relative error of at most 0.00012.
Values sent between devices are 32-bit elements; how exact they have to be, the bound alone decides.
No kernel may reach another device: no remote copies, remote signals or barrier semaphores. Data moves between devices by JAX's collectives and lax.ppermute only.
A program may use at most 64 MiB of HBM per device.

```python
import math
import jax
import jax.numpy as jnp
from jax import lax

MEMBERS = 12
VARS = 3
STEPS = 8
NLON = 1024
NLAT = 64


def draw_perturbations(key, part):
    keys = jax.random.split(key, 3)
    shape = (MEMBERS, 3, NLAT, NLON)
    values = jnp.clip(jax.random.normal(keys[0], shape, jnp.float32), -4.0, 4.0)
    cells = jnp.exp(math.log(10.0) * jax.random.uniform(keys[1], (1, 3, NLAT, NLON), jnp.float32))
    columns = jnp.exp(math.log(10.0) * jax.random.uniform(keys[2], (MEMBERS, 1, 1, 1), jnp.float32))
    rise_lat = 1.0 + jnp.arange(NLAT, dtype=jnp.float32) / NLAT
    rise_lon = 1.0 + jnp.arange(NLON, dtype=jnp.float32) / NLON
    rise = rise_lat[:, None] * rise_lon[None, :]
    return (values * cells * columns * rise).astype(jnp.float32)


def block_levels(own_key, dims, cuts, smallest, high):
    def one(dim, parts):
        steps = jax.random.uniform(jax.random.fold_in(jax.random.fold_in(own_key, 6), dim), (parts,), jnp.float32, smallest / len(cuts), high / len(cuts))
        return jnp.repeat(jnp.exp(steps), dims[dim] // parts).reshape((-1,) + (1,) * (len(dims) - dim - 1))

    gain = one(*cuts[0])
    for cut in cuts[1:]:
        gain = gain * one(*cut)
    return gain


def normal_values(key, shape, spread, bound, cuts=(), kind=jnp.bfloat16):
    level = block_levels(key, shape, cuts, -0.22, 0.18) if cuts else 1.0
    values = jax.random.normal(key, shape, jnp.float32) * spread * level
    return jnp.minimum(jnp.maximum(values, -bound), bound).astype(kind)


def setup_inputs(seed: int = 0) -> dict:
    streams_of = jax.random.split(jax.random.key(seed), 4)
    return {
        "perturbations": draw_perturbations(jax.random.fold_in(streams_of[3], 71), 0),
        "base_wind": normal_values(streams_of[1], (2, NLAT, NLON), 1.0, 4.0, ((1, 4), (2, 8)), jnp.float32),
        "base_height": jnp.clip(0.5 + 1.0 * jax.random.uniform(streams_of[2], (NLAT, NLON), jnp.float32) ** block_levels(streams_of[2], (NLAT, NLON), ((0, 4), (1, 8)), -0.2, 0.2), 0.5, 1.5),
    }


advect_rate = 0.1
turn_rate = 0.5
gravity_rate = 0.2
diffuse_rate = 0.12

def centre(array):
    return array[..., 1:-1, 1:-1]

def diff_lon(array):
    return 0.5 * (array[..., 1:-1, 2:] - array[..., 1:-1, :-2])

def diff_lat(array):
    return 0.5 * (array[..., 2:, 1:-1] - array[..., :-2, 1:-1])

def laplacian(array):
    return array[..., 2:, 1:-1] + array[..., :-2, 1:-1] + array[..., 1:-1, 2:] + array[..., 1:-1, :-2] - 4.0 * centre(array)

def advance(field, base, turning):
    wind_x = field[..., 0, :, :]
    wind_y = field[..., 1, :, :]
    height = field[..., 2, :, :]
    base_x = base[0]
    base_y = base[1]
    base_depth = base[2]
    mean_x = centre(base_x)
    mean_y = centre(base_y)
    inner_x = centre(wind_x)
    inner_y = centre(wind_y)
    new_x = inner_x - advect_rate * (mean_x * diff_lon(wind_x) + inner_x * diff_lon(base_x) + mean_y * diff_lat(wind_x) + inner_y * diff_lat(base_x)) + turn_rate * turning * inner_y - gravity_rate * diff_lon(height) + diffuse_rate * laplacian(wind_x)
    new_y = inner_y - advect_rate * (mean_x * diff_lon(wind_y) + inner_x * diff_lon(base_y) + mean_y * diff_lat(wind_y) + inner_y * diff_lat(base_y)) - turn_rate * turning * inner_x - gravity_rate * diff_lat(height) + diffuse_rate * laplacian(wind_y)
    new_height = centre(height) - advect_rate * (diff_lon(base_depth * wind_x + height * base_x) + diff_lat(base_depth * wind_y + height * base_y)) + diffuse_rate * laplacian(height)
    return jnp.stack([new_x, new_y, new_height], axis=-3)

def coriolis(start, rows, total):
    glob = (start + jnp.arange(rows, dtype=jnp.int32)).astype(jnp.float32)
    return jnp.sin(math.pi * ((glob + 0.5) / total - 0.5))[:, None]

def extend_grid(array, width):
    lead = [(0, 0)] * (array.ndim - 2)
    wrapped = jnp.pad(array, lead + [(0, 0), (width, width)], mode='wrap')
    return jnp.pad(wrapped, lead + [(width, width), (0, 0)])

def reference(perturbations, base_wind, base_height):
    base = jnp.concatenate([base_wind, base_height[None]], axis=0)
    base_ext = extend_grid(base, 1)
    turning = coriolis(0, NLAT, NLAT)

    def evolve(member):
        for step_index in range(STEPS):
            member = advance(extend_grid(member, 1), base_ext, turning)
        return member
    evolved = lax.map(evolve, perturbations)
    flattened = evolved.reshape(MEMBERS, -1)
    cell_count = float(VARS * NLAT * NLON)
    gram = jnp.dot(flattened, flattened.T, precision=lax.Precision.HIGHEST) / cell_count
    lower_factor = jnp.linalg.cholesky(gram)
    fields = jax.scipy.linalg.solve_triangular(lower_factor, flattened, lower=True)
    return (fields.reshape(perturbations.shape), lower_factor.T)
```

```python
import functools
import math

import jax
import jax.numpy as jnp
from jax import lax
from jax.experimental import pallas as pl
from jax.experimental.pallas import tpu as pltpu
from jax.sharding import PartitionSpec as P

STEPS = 8
HALO = STEPS
LANES = 128
PLANE = 40
STRIP = 3 * HALO
SLOTS = LANES // STRIP
NCOEF = 18

advect_rate = 0.1
turn_rate = 0.5
gravity_rate = 0.2
diffuse_rate = 0.12

VMEM = pl.BlockSpec(memory_space=pltpu.VMEM)
PARAMS = pltpu.CompilerParams(vmem_limit_bytes=32 * 1024 * 1024)


def shift_e(x):
    return pltpu.roll(x, x.shape[-1] - 1, axis=x.ndim - 1)


def shift_w(x):
    return pltpu.roll(x, 1, axis=x.ndim - 1)


def rotate(x, amount):
    amount = amount % LANES
    return x if amount == 0 else pltpu.roll(x, amount, axis=x.ndim - 1)


def lane_ids(rows):
    return lax.broadcasted_iota(jnp.int32, (rows, LANES), 1)


def dynamic_zero():
    return jnp.minimum(lax.axis_index("lat"), 0)


def store_coefs(base, offset, rows_ref, coef, coef_offset):
    half_a = 0.5 * advect_rate
    for t in range(4):
        m = rows_ref[0, 8 * t : 8 * t + 8, :]
        turn = rows_ref[1, 8 * t : 8 * t + 8, :]

        def three(v):
            start = offset + v * PLANE + 8 * t
            return [base[pl.ds(start + d, 8), :] for d in range(3)]

        us, u, un = three(0)
        vs, v, vn = three(1)
        hs, h, hn = three(2)
        ue, uw, ve, vw, he, hw = shift_e(u), shift_w(u), shift_e(v), shift_w(v), shift_e(h), shift_w(h)
        centre = (1.0 - 4.0 * diffuse_rate) * m
        dif = diffuse_rate * m
        am = half_a * m
        values = [
            dif - am * u,
            dif + am * u,
            dif - am * v,
            dif + am * v,
            centre - am * (ue - uw),
            turn - am * (un - us),
            centre - am * (vn - vs),
            -turn - am * (ve - vw),
            (0.5 * gravity_rate) * m,
            dif - am * ue,
            dif + am * uw,
            dif - am * vn,
            dif + am * vs,
            -am * he,
            am * hw,
            -am * hn,
            am * hs,
            centre,
        ]
        for i, value in enumerate(values):
            coef[pl.ds(coef_offset + i * PLANE + 8 * t, 8), :] = value


def tiles_of(step):
    return -(-(32 - 2 * step) // 8)


def advance(src, dst, step, groups):
    for t in range(tiles_of(step)):
        for coef, coef_offset, triples in groups:
            (ae, aw, an, as_, cu, du, cv, dv, k1, he, hw, hn, hs, ue, uw, vn, vs, c0) = [
                coef[pl.ds(coef_offset + i * PLANE + 8 * t + step - 1, 8), :] for i in range(NCOEF)
            ]
            for offset in triples:

                def three(v):
                    start = offset + v * PLANE + 8 * t
                    return [src[pl.ds(start + d, 8), :] for d in range(3)]

                u_s, u, u_n = three(0)
                v_s, v, v_n = three(1)
                h_s, h, h_n = three(2)
                u_e, u_w = shift_e(u), shift_w(u)
                v_e, v_w = shift_e(v), shift_w(v)
                h_e, h_w = shift_e(h), shift_w(h)
                new_u = (
                    (ae * u_e + aw * u_w) + (an * u_n + as_ * u_s) + (cu * u + du * v) + k1 * (h_w - h_e)
                )
                new_v = (
                    (ae * v_e + aw * v_w) + (an * v_n + as_ * v_s) + (cv * v + dv * u) + k1 * (h_s - h_n)
                )
                new_h = (
                    (he * h_e + hw * h_w)
                    + (hn * h_n + hs * h_s)
                    + (ue * u_e + uw * u_w)
                    + (vn * v_n + vs * v_s)
                    + c0 * h
                )
                dst[pl.ds(offset + 8 * t, 8), :] = new_u
                dst[pl.ds(offset + PLANE + 8 * t, 8), :] = new_v
                dst[pl.ds(offset + 2 * PLANE + 8 * t, 8), :] = new_h


def parity(axis):
    return lax.rem(lax.axis_index(axis), 2) == 0


def pack_kernel(members, pert, wind, height, recv_a, recv_b, msg_a, msg_b):
    lat_even = parity("lat")
    lon_even = parity("lon")
    lanes8 = lane_ids(8)
    for v in range(3):
        for piece in range(4):
            pack_e = None
            for m in range(members + 1):
                if piece in (1, 2):
                    rows = slice(8 * piece - 8, 8 * piece)
                    if m < members:
                        x = pert[m, v, rows, :]
                    elif v < 2:
                        x = wind[v, rows, :]
                    else:
                        x = height[rows, :]
                else:
                    north = lat_even if piece == 0 else jnp.logical_not(lat_even)
                    x = jnp.where(north, recv_b[m, v], recv_a[m, v])
                to_w = rotate(x, HALO * m)
                to_e = rotate(x, HALO * m + HALO)
                if m == 0:
                    pack_w, pack_e = to_w, to_e
                else:
                    here = lanes8 >= HALO * m
                    pack_w = jnp.where(here, to_w, pack_w)
                    pack_e = jnp.where(here, to_e, pack_e)
            rows = slice(8 * piece, 8 * piece + 8)
            msg_a[v, rows, :] = jnp.where(lon_even, pack_e, pack_w)
            msg_b[v, rows, :] = jnp.where(lon_even, pack_w, pack_e)


def strip_places(members):
    full = members // SLOTS
    left = members - full * SLOTS
    places = {}
    sets = []
    for side in (0, 1):
        for g in range(full):
            for s in range(SLOTS):
                places[(g * SLOTS + s, side)] = (len(sets), s)
            sets.append(side)
    for r in range(left):
        places[(full * SLOTS + r, 0)] = (len(sets), r)
        places[(full * SLOTS + r, 1)] = (len(sets), left + r)
    sets.append(2)
    return places, sets, left


def centre_kernel(
    members, pert, wind, height, recv_a, recv_b, rows_ref, centre, strips, base_strips, first, second, base, coef
):
    zero = dynamic_zero()
    lat_even = parity("lat")
    off_a = pl.multiple_of(jnp.where(lat_even, 24, 0), 8)
    off_b = pl.multiple_of(jnp.where(lat_even, 0, 24), 8)
    for m in range(members + 1):
        for v in range(3):
            if m < members:
                plane, own = first, pert[m, v]
                start = (3 * m + v) * PLANE
            else:
                plane, own = base, (wind[v] if v < 2 else height[...])
                start = v * PLANE
            plane[start + 8 : start + 24, :] = own
            plane[pl.ds(start + off_a, 8), :] = recv_a[m, v]
            plane[pl.ds(start + off_b, 8), :] = recv_b[m, v]
    store_coefs(base, zero, rows_ref, coef, zero)

    places, sets, left = strip_places(members)
    lanes8 = lane_ids(8)
    for v in range(3):
        for t in range(4):
            rows = slice(8 * t, 8 * t + 8)
            groups = [None] * len(sets)
            for m in range(members):
                start = (3 * m + v) * PLANE + 8 * t
                x = first[start : start + 8, :]
                for side in (0, 1):
                    g, s = places[(m, side)]
                    moved = rotate(x, STRIP * s + (HALO if side == 0 else 2 * HALO))
                    if groups[g] is None:
                        groups[g] = moved
                    else:
                        here = (lanes8 >= STRIP * s) & (lanes8 < STRIP * s + STRIP)
                        groups[g] = jnp.where(here, moved, groups[g])
            for g in range(len(sets)):
                strips[v, g, rows, :] = groups[g]
            start = v * PLANE + 8 * t
            x = base[start : start + 8, :]
            for side in (0, 1):
                acc = None
                for s in range(SLOTS):
                    moved = rotate(x, STRIP * s + (HALO if side == 0 else 2 * HALO))
                    acc = moved if s == 0 else jnp.where(lanes8 >= STRIP * s, moved, acc)
                base_strips[v, side, rows, :] = acc

    per_iter = 3

    def some_members(i, carry):
        offsets = [(i * per_iter + j) * (3 * PLANE) for j in range(per_iter)]
        refs = [first, second]
        for step in range(1, STEPS + 1):
            advance(refs[(step - 1) % 2], refs[step % 2], step, [(coef, zero, offsets)])
        for j in range(per_iter):
            for v in range(3):
                centre[i * per_iter + j, v] = refs[STEPS % 2][pl.ds(offsets[j] + v * PLANE, 16), :]
        return carry

    lax.fori_loop(0, members // per_iter, some_members, 0)


def strips_kernel(
    members, centre, strips, base_strips, got_a, got_b, rows_ref, fields, send, first, second, base, coef, pairs
):
    zero = dynamic_zero()
    lon_even = parity("lon")
    places, sets, left = strip_places(members)
    lanes8 = lane_ids(8)
    in_strip = lax.rem(lanes8, STRIP)
    for v in range(3):
        for t in range(4):
            rows = slice(8 * t, 8 * t + 8)
            a, b = got_a[v, rows, :], got_b[v, rows, :]
            halos = [jnp.where(lon_even, b, a), jnp.where(lon_even, a, b)]
            groups = [strips[v, g, rows, :] for g in range(len(sets))]
            for m in range(members):
                for side in (0, 1):
                    g, s = places[(m, side)]
                    low = STRIP * s + (0 if side == 0 else 2 * HALO)
                    moved = rotate(halos[side], low - HALO * m)
                    groups[g] = jnp.where((lanes8 >= low) & (lanes8 < low + HALO), moved, groups[g])
            for g in range(len(sets)):
                start = (3 * g + v) * PLANE + 8 * t
                first[start : start + 8, :] = groups[g]
            basis = []
            for side in (0, 1):
                acc = None
                for s in range(SLOTS):
                    moved = rotate(halos[side], STRIP * s + (0 if side == 0 else 2 * HALO) - HALO * members)
                    acc = moved if s == 0 else jnp.where(lanes8 >= STRIP * s, moved, acc)
                here = (in_strip < HALO) if side == 0 else (in_strip >= 2 * HALO)
                basis.append(jnp.where(here, acc, base_strips[v, side, rows, :]))
            basis.append(jnp.where(lanes8 < STRIP * left, basis[0], basis[1]))
            for kind in range(3):
                start = (3 * kind + v) * PLANE + 8 * t
                base[start : start + 8, :] = basis[kind]
    for kind in range(3):
        store_coefs(base, zero + kind * 3 * PLANE, rows_ref, coef, zero + kind * NCOEF * PLANE)
    refs = [first, second]
    work = [
        (coef, zero + kind * NCOEF * PLANE, [zero + g * 3 * PLANE for g in range(len(sets)) if sets[g] == kind])
        for kind in range(3)
    ]
    for step in range(1, STEPS + 1):
        advance(refs[(step - 1) % 2], refs[step % 2], step, work)
    done = refs[STEPS % 2]
    lanes16 = lane_ids(16)
    for m in range(members):
        for v in range(3):
            x = centre[m, v]
            for side in (0, 1):
                g, s = places[(m, side)]
                start = (3 * g + v) * PLANE
                moved = rotate(done[start : start + 16, :], (0 if side == 0 else LANES - HALO) - STRIP * s - HALO)
                here = (lanes16 < HALO) if side == 0 else (lanes16 >= LANES - HALO)
                x = jnp.where(here, moved, x)
            fields[m, v] = x
    pairs[...] = jnp.zeros_like(pairs)
    index = 0
    for i in range(members):
        for j in range(i, members):
            total = None
            for v in range(3):
                prod = fields[i, v] * fields[j, v]
                part = prod[:8] + prod[8:]
                total = part if total is None else total + part
            pairs[8 * index : 8 * index + 8, :] = total
            index += 1
    partial = pairs[pl.ds(0, LANES, stride=8), :]
    for s in range(1, 8):
        partial = partial + pairs[pl.ds(s, LANES, stride=8), :]
    row = jnp.sum(partial.T, axis=0, keepdims=True)
    send[...] = jnp.broadcast_to(row, send.shape)


def final_kernel(members, count, fields, got, out, factor):
    total = got[0:8, :]
    for r in range(8, got.shape[0], 8):
        total = total + got[r : r + 8, :]
    packed = jnp.sum(total, axis=0, keepdims=True) / count
    packed = jnp.broadcast_to(packed, (8, LANES))
    rows = []
    at = 0
    for i in range(members):
        rows.append(rotate(packed, i - at))
        at += members - i
    x = [[fields[m, v] for v in range(3)] for m in range(members)]
    lanes8 = lane_ids(8)
    for k in range(members):
        spread = [
            jnp.broadcast_to(rows[k][:, i : i + 1], (8, LANES)) if i >= k else None for i in range(members)
        ]
        inverse = 1.0 / spread[k]
        scale = lax.rsqrt(spread[k])
        scale16 = jnp.concatenate([scale, scale], axis=0)
        for v in range(3):
            out[k, v] = x[k][v] * scale16
        kept = (lanes8 >= k) & (lanes8 < members)
        factor[k : k + 1, :] = jnp.where(kept, rows[k] * scale, 0.0)[0:1, :members]
        for i in range(k + 1, members):
            times = spread[i] * inverse
            rows[i] = rows[i] - times * rows[k]
            times16 = jnp.concatenate([times, times], axis=0)
            for v in range(3):
                x[i][v] = x[i][v] - times16 * x[k][v]


def swap(block, axis, count, even_up, periodic):
    pairs = []
    for i in range(count):
        other = i + 1 if (i % 2 == 0) == even_up else i - 1
        if periodic:
            other %= count
        if 0 <= other < count:
            pairs.append((i, other))
    return lax.ppermute(block, axis, pairs)


def per_device(perturbations, base_wind, base_height):
    members, _, rows, cols = perturbations.shape
    n_lat, n_lon = lax.axis_size("lat"), lax.axis_size("lon")
    devices = n_lat * n_lon
    total_rows = rows * n_lat
    total_cols = cols * n_lon
    f32 = jnp.float32

    glob = lax.axis_index("lat") * rows - HALO + 1 + jnp.arange(PLANE, dtype=jnp.int32)
    inside = ((glob >= 0) & (glob < total_rows)).astype(f32)
    turning = turn_rate * inside * jnp.sin(math.pi * ((glob.astype(f32) + 0.5) / total_rows - 0.5))
    row_facts = jnp.broadcast_to(jnp.stack([inside, turning])[:, :, None], (2, PLANE, LANES))

    base = jnp.concatenate([base_wind, base_height[None]], axis=0)
    everything = jnp.concatenate([perturbations, base[None]], axis=0)
    top, bottom = everything[:, :, :HALO], everything[:, :, rows - HALO :]
    lat_even = lax.axis_index("lat") % 2 == 0
    recv_b = swap(jnp.where(lat_even, top, bottom), "lat", n_lat, False, False)
    recv_a = swap(jnp.where(lat_even, bottom, top), "lat", n_lat, True, False)

    message = jax.ShapeDtypeStruct((3, 32, LANES), f32)
    msg_a, msg_b = pl.pallas_call(
        functools.partial(pack_kernel, members),
        out_shape=[message, message],
        in_specs=[VMEM] * 5,
        out_specs=[VMEM] * 2,
        compiler_params=PARAMS,
        name="pack",
    )(perturbations, base_wind, base_height, recv_a, recv_b)
    got_b = swap(msg_b, "lon", n_lon, False, True)
    got_a = swap(msg_a, "lon", n_lon, True, True)

    _, sets, _ = strip_places(members)
    groups = len(sets)
    centre, strips, base_strips = pl.pallas_call(
        functools.partial(centre_kernel, members),
        out_shape=[
            jax.ShapeDtypeStruct(perturbations.shape, f32),
            jax.ShapeDtypeStruct((3, groups, 32, LANES), f32),
            jax.ShapeDtypeStruct((3, 2, 32, LANES), f32),
        ],
        in_specs=[VMEM] * 6,
        out_specs=[VMEM] * 3,
        scratch_shapes=[
            pltpu.VMEM((members * 3 * PLANE, LANES), f32),
            pltpu.VMEM((members * 3 * PLANE, LANES), f32),
            pltpu.VMEM((3 * PLANE, LANES), f32),
            pltpu.VMEM((NCOEF * PLANE, LANES), f32),
        ],
        compiler_params=PARAMS,
        cost_estimate=pl.CostEstimate(flops=20_000_000, bytes_accessed=2_000_000, transcendentals=0),
        name="centre",
    )(perturbations, base_wind, base_height, recv_a, recv_b, row_facts)

    fields, send = pl.pallas_call(
        functools.partial(strips_kernel, members),
        out_shape=[
            jax.ShapeDtypeStruct(perturbations.shape, f32),
            jax.ShapeDtypeStruct((devices, LANES), f32),
        ],
        in_specs=[VMEM] * 6,
        out_specs=[VMEM] * 2,
        scratch_shapes=[
            pltpu.VMEM((groups * 3 * PLANE, LANES), f32),
            pltpu.VMEM((groups * 3 * PLANE, LANES), f32),
            pltpu.VMEM((3 * 3 * PLANE, LANES), f32),
            pltpu.VMEM((3 * NCOEF * PLANE, LANES), f32),
            pltpu.VMEM((8 * LANES, LANES), f32),
        ],
        compiler_params=PARAMS,
        name="edges",
    )(centre, strips, base_strips, got_a, got_b, row_facts)

    got = lax.all_to_all(send, ("lon", "lat"), 0, 0, tiled=True)

    return pl.pallas_call(
        functools.partial(final_kernel, members, float(3 * total_rows * total_cols)),
        out_shape=[
            jax.ShapeDtypeStruct(perturbations.shape, f32),
            jax.ShapeDtypeStruct((members, members), f32),
        ],
        in_specs=[VMEM] * 2,
        out_specs=[VMEM] * 2,
        compiler_params=PARAMS,
        name="finish",
    )(fields, got)


def solution(mesh):
    return jax.shard_map(
        per_device,
        mesh=mesh,
        in_specs=(P(None, None, "lat", "lon"), P(None, "lat", "lon"), P("lat", "lon")),
        out_specs=(P(None, None, "lat", "lon"), P()),
        check_vma=False,
    )
```

```python
import functools
import math

import jax
import jax.numpy as jnp
from jax import lax
from jax.experimental import pallas as pl
from jax.experimental.pallas import tpu as pltpu
from jax.sharding import PartitionSpec as P

STEPS = 8
HALO = STEPS
TILE = 8
LANES = 128
FACTS = 40
STRIP = 3 * HALO
SLOTS = LANES // STRIP
MIX = 2 * STRIP + HALO
KINDS = 3
NCOEF = 18

advect_rate = 0.1
turn_rate = 0.5
gravity_rate = 0.2
diffuse_rate = 0.12

f32 = jnp.float32
VMEM = pl.BlockSpec(memory_space=pltpu.VMEM)
HBM = pl.BlockSpec(memory_space=pltpu.HBM)
PARAMS = pltpu.CompilerParams(vmem_limit_bytes=40 * 1024 * 1024)


def rotate(x, amount):
    amount = amount % LANES
    return x if amount == 0 else pltpu.roll(x, amount, axis=x.ndim - 1)


def lane_ids(rows=TILE):
    return lax.broadcasted_iota(jnp.int32, (rows, LANES), 1)


def dynamic_zero():
    return jnp.minimum(lax.axis_index("lat"), 0)


def is_even(axis):
    return lax.rem(lax.axis_index(axis), 2) == 0


def store_coefs(base, at, stride, facts, facts_at, coef, coef_at, tiles):
    half = 0.5 * advect_rate
    for t in tiles:
        m = facts[0, pl.ds(facts_at + TILE * t, TILE), :]
        turn = facts[1, pl.ds(facts_at + TILE * t, TILE), :]

        def three(v):
            return [base[pl.ds(at + v * stride + TILE * t + d, TILE), :] for d in range(3)]

        us, u, un = three(0)
        vs, v, vn = three(1)
        hs, h, hn = three(2)
        ue, ve, he = rotate(u, -1), rotate(v, -1), rotate(h, -1)
        uw, vw, hw = rotate(u, 1), rotate(v, 1), rotate(h, 1)
        centre = (1.0 - 4.0 * diffuse_rate) * m
        dif = diffuse_rate * m
        am = half * m
        values = [
            dif - am * u,
            dif + am * u,
            dif - am * v,
            dif + am * v,
            centre - am * (ue - uw),
            turn - am * (un - us),
            centre - am * (vn - vs),
            -turn - am * (ve - vw),
            (0.5 * gravity_rate) * m,
            dif - am * ue,
            dif + am * uw,
            dif - am * vn,
            dif + am * vs,
            -am * he,
            am * hw,
            -am * hn,
            am * hs,
            centre,
        ]
        for i, value in enumerate(values):
            coef[pl.ds(coef_at + i * FACTS + TILE * t, TILE), :] = value


def load_coefs(coef, at):
    return [coef[pl.ds(at + i * FACTS, TILE), :] for i in range(NCOEF)]


def step_tile(src, at, stride, coefs):
    (ae, aw, an, as_, cu, du, cv, dv, k1, he, hw, hn, hs, ue, uw, vn, vs, c0) = coefs

    def three(v):
        return [src[pl.ds(at + v * stride + d, TILE), :] for d in range(3)]

    u_s, u, u_n = three(0)
    v_s, v, v_n = three(1)
    h_s, h, h_n = three(2)
    u_e, v_e, h_e = rotate(u, -1), rotate(v, -1), rotate(h, -1)
    u_w, v_w, h_w = rotate(u, 1), rotate(v, 1), rotate(h, 1)
    new_u = (ae * u_e + aw * u_w) + (an * u_n + as_ * u_s) + (cu * u + du * v) + k1 * (h_w - h_e)
    new_v = (ae * v_e + aw * v_w) + (an * v_n + as_ * v_s) + (cv * v + dv * u) + k1 * (h_s - h_n)
    new_h = (he * h_e + hw * h_w) + (hn * h_n + hs * h_s) + (ue * u_e + uw * u_w) + (vn * v_n + vs * v_s) + c0 * h
    return new_u, new_v, new_h


PYRAMID = 24
FRONT = 8


def pyramid(refs, zero, work, hist):
    def keep(step, source, plane):
        start = zero + FRONT + plane * PYRAMID
        hist[0, step, plane] = source[pl.ds(start, TILE), :]
        hist[1, step, plane] = source[pl.ds(start + TILE - 2 * step, TILE), :]

    for step in range(1, STEPS):
        src, dst = refs[(step - 1) % 2], refs[step % 2]
        for t in range(-(-(16 - 2 * step) // TILE)):
            for coef, coef_at, triples in work:
                coefs = load_coefs(coef, coef_at + TILE * t + step - 1)
                for triple in triples:
                    at = FRONT + 3 * triple * PYRAMID + TILE * t
                    new = step_tile(src, zero + at, PYRAMID, coefs)
                    for v in range(3):
                        dst[pl.ds(zero + at + v * PYRAMID, TILE), :] = new[v]
        for _, _, triples in work:
            for triple in triples:
                for v in range(3):
                    keep(step, dst, 3 * triple + v)


def first_level(hist, plane, low, high):
    hist[0, 0, plane] = low
    hist[1, 0, plane] = high


def slot_range(s, shift):
    lanes = (lane_ids() + shift) % LANES
    return (lanes >= STRIP * s) & (lanes < STRIP * s + STRIP)


def in_strip():
    return lane_ids() % STRIP


def own_strips(rows_of, members):
    vectors = []
    for q in range(-(-members // SLOTS)):
        west = east = None
        for s in range(min(SLOTS, members - SLOTS * q)):
            moved = rotate(rows_of(SLOTS * q + s), STRIP * s + HALO)
            west = moved if s == 0 else jnp.where(slot_range(s, 0), moved, west)
            east = moved if s == 0 else jnp.where(slot_range(s, HALO), moved, east)
        vectors.append((west, east))
    return vectors


def base_own_strips(rows):
    west = east = None
    for s in range(SLOTS):
        moved = rotate(rows, STRIP * s + HALO)
        west = moved if s == 0 else jnp.where(slot_range(s, 0), moved, west)
        east = moved if s == 0 else jnp.where(slot_range(s, HALO), moved, east)
    return west, east


def mix(west, east):
    return jnp.where(lane_ids() < 2 * STRIP, west, rotate(east, MIX))


def fill_strips(vectors, west_halo, east_halo):
    place = in_strip()
    wests, easts = [], []
    for q, (west, east) in enumerate(vectors):
        wests.append(jnp.where(place < HALO, rotate(west_halo, -HALO * q), west))
        here = (place >= HALO) & (place < 2 * HALO)
        easts.append(jnp.where(here, rotate(east_halo, -HALO * q), east))
    return wests[:-1] + easts[:-1] + [mix(wests[-1], easts[-1])]


def base_strips(rows, west_halo, east_halo, members):
    q, first = members // SLOTS, members % SLOTS
    place = in_strip()
    west, east = base_own_strips(rows)

    def everywhere(halo, edge):
        near = rotate(halo, -HALO * q)
        return jnp.where(lane_ids() < STRIP * first + edge, rotate(near, -STRIP * first), near)

    west = jnp.where(place < HALO, everywhere(west_halo, 0), west)
    here = (place >= HALO) & (place < 2 * HALO)
    east = jnp.where(here, everywhere(east_halo, HALO), east)
    return west, east, mix(west, east)


def strip_kinds(members):
    full = members // SLOTS
    return [0] * full + [1] * full + [2]


def load_kernel(members, pert, wind, height, own, msg_a, msg_b, sems):
    chunk = members // 4
    copies = [
        pltpu.make_async_copy(wind, own.at[members, pl.ds(0, 2)], sems.at[0]),
        pltpu.make_async_copy(height, own.at[members, 2], sems.at[1]),
    ]
    for i in range(4):
        part = pl.ds(i * chunk, chunk)
        copies.append(pltpu.make_async_copy(pert.at[part], own.at[part], sems.at[2 + i]))
    for copy in copies:
        copy.start()
    for copy in copies:
        copy.wait()
    lon_even = is_even("lon")
    lanes = lane_ids()
    for v in range(3):
        for t in range(2):
            rows = slice(TILE * t, TILE * t + TILE)
            to_e = to_w = None
            for q in range(3):
                for s in range(SLOTS):
                    low = STRIP * s + HALO * q
                    moved = rotate(own[min(SLOTS * q + s, members), v, rows, :], low + HALO)
                    if to_e is None:
                        to_e = to_w = moved
                    else:
                        to_e = jnp.where((lanes >= low) & (lanes < low + HALO), moved, to_e)
                        to_w = jnp.where((lanes >= low + HALO) & (lanes < low + 2 * HALO), moved, to_w)
            msg_a[v, rows, :] = jnp.where(lon_even, to_e, to_w)
            msg_b[v, rows, :] = jnp.where(lon_even, to_w, to_e)


def centre_kernel(members, total_rows, own, facts, hist, first, second, base, coef):
    zero = dynamic_zero()
    start = lax.axis_index("lat") * 16 - HALO + 1
    for t in range(FACTS // TILE):
        glob = start + TILE * t + lax.broadcasted_iota(jnp.int32, (TILE, LANES), 0)
        inside = ((glob >= 0) & (glob < total_rows)).astype(f32)
        rows = slice(TILE * t, TILE * t + TILE)
        facts[0, rows, :] = inside
        facts[1, rows, :] = turn_rate * inside * jnp.sin(math.pi * ((glob.astype(f32) + 0.5) / total_rows - 0.5))
    for m in range(members + 1):
        for v in range(3):
            low, high = own[m, v, 0:TILE, :], own[m, v, TILE:16, :]
            plane = 3 * m + v
            if m < members:
                ref, at = first, FRONT + plane * PYRAMID
                first_level(hist, plane, low, high)
            else:
                ref, at = base, FRONT + v * PYRAMID
            ref[at : at + TILE, :] = low
            ref[at + TILE : at + 16, :] = high
    store_coefs(base, zero + FRONT, PYRAMID, facts, HALO, coef, zero, range(2))
    pyramid([first, second], zero, [(coef, zero, list(range(members)))], hist)


def meet_kernel(members, own, got_a, got_b, send_a, send_b, west, east):
    lat_even, lon_even = is_even("lat"), is_even("lon")
    low = pl.multiple_of(jnp.where(lat_even, TILE, 0), TILE)
    for send, at in ((send_a, low), (send_b, TILE - low)):
        at = pl.multiple_of(at, TILE)
        for m in range(members + 1):
            for v in range(3):
                send[3 * m + v] = own[m, v, pl.ds(at, TILE), :]
        for v in range(3):
            a, b = got_a[v, pl.ds(at, TILE), :], got_b[v, pl.ds(at, TILE), :]
            send[3 * members + 3 + v] = jnp.where(lon_even, b, a)
            send[3 * members + 6 + v] = jnp.where(lon_even, a, b)
    for v in range(3):
        for t in range(2):
            rows = slice(TILE * t, TILE * t + TILE)
            west[v, rows, :] = jnp.where(lon_even, got_b[v, rows, :], got_a[v, rows, :])
            east[v, rows, :] = jnp.where(lon_even, got_a[v, rows, :], got_b[v, rows, :])


def edges_kernel(members, own, west, east, facts, hist, strip_base, first, second, base, coef):
    zero = dynamic_zero()
    kinds = strip_kinds(members)
    for v in range(3):
        for t in range(2):
            rows = slice(TILE * t, TILE * t + TILE)
            halos = west[v, rows, :], east[v, rows, :]
            strips = fill_strips(own_strips(lambda m: own[m, v, rows, :], members), *halos)
            for g, strip in enumerate(strips):
                at = FRONT + (3 * g + v) * PYRAMID + TILE * t
                first[at : at + TILE, :] = strip
                hist[t, 0, 3 * g + v] = strip
            for kind, strip in enumerate(base_strips(own[members, v, rows, :], *halos, members)):
                at = FRONT + (3 * kind + v) * PYRAMID + TILE * t
                base[at : at + TILE, :] = strip
                strip_base[kind, v, rows, :] = strip
    work = []
    for kind in range(KINDS):
        coef_at = zero + kind * NCOEF * FACTS
        store_coefs(base, zero + FRONT + 3 * kind * PYRAMID, PYRAMID, facts, HALO, coef, coef_at, range(2))
        work.append((coef, coef_at, [g for g in range(len(kinds)) if kinds[g] == kind]))
    pyramid([first, second], zero, work, hist)


WEDGE = 16
BASE = 40


def side_kernel(
    members, is_a, own, halo, facts, hist_c, hist_e, strip_base, partial_in, fields, result, *scratch
):
    base, base_e, coef, coef_e, pairs = scratch[:5]
    count = (len(scratch) - 5) // 2
    first, second = scratch[5 : 5 + count], scratch[5 + count :]
    north = jnp.logical_not(is_even("lat")) if is_a else is_even("lat")
    side = jnp.where(north, 0, 1)
    wedge_at = jnp.where(north, 0, TILE)
    hist_at = jnp.where(north, TILE, 0)
    read_at = jnp.where(north, 0, TILE - 2)
    own_at = jnp.where(north, 2 * TILE, 1)
    halo_at = jnp.where(north, TILE, 2 * TILE + 1)
    facts_at = jnp.where(north, 0, 2 * TILE - 1)
    zero = dynamic_zero()
    kinds = strip_kinds(members)
    groups = len(kinds)
    triples_c = list(range(members))
    planes_c = 3 * members

    for m in range(members):
        for v in range(3):
            first[m][pl.ds(wedge_at + v * WEDGE, TILE), :] = halo[3 * m + v]
    for v in range(3):
        west, east = halo[planes_c + 3 + v], halo[planes_c + 6 + v]
        strips = fill_strips(own_strips(lambda m: halo[3 * m + v], members), west, east)
        for g, strip in enumerate(strips):
            first[members + g][pl.ds(wedge_at + v * WEDGE, TILE), :] = strip
        for t in range(2):
            base[pl.ds(own_at + v * BASE + TILE * t, TILE), :] = own[members, v, TILE * t : TILE * t + TILE, :]
        base[pl.ds(halo_at + v * BASE, TILE), :] = halo[planes_c + v]
        for kind, strip in enumerate(base_strips(halo[planes_c + v], west, east, members)):
            plane = 3 * kind + v
            for t in range(2):
                base_e[pl.ds(own_at + plane * BASE + TILE * t, TILE), :] = strip_base[
                    kind, v, TILE * t : TILE * t + TILE, :
                ]
            base_e[pl.ds(halo_at + plane * BASE, TILE), :] = strip
    store_coefs(base, zero + TILE, BASE, facts, facts_at, coef, zero, range(2))
    work = [(coef, zero, triples_c)]
    for kind in range(KINDS):
        coef_at = zero + kind * NCOEF * FACTS
        store_coefs(base_e, zero + TILE + 3 * kind * BASE, BASE, facts, facts_at, coef_e, coef_at, range(2))
        work.append((coef_e, coef_at, [members + g for g in range(groups) if kinds[g] == kind]))

    refs = [first, second]

    def lean(step):
        for triple, ref in enumerate(refs[step % 2]):
            for v in range(3):
                if triple < members:
                    rows = hist_c[side, step, 3 * triple + v]
                else:
                    rows = hist_e[side, step, 3 * (triple - members) + v]
                ref[pl.ds(hist_at + v * WEDGE, TILE), :] = rows

    lean(0)
    for step in range(1, STEPS + 1):
        src, dst = refs[(step - 1) % 2], refs[step % 2]
        row = jnp.where(north, step - 1, STEPS - step)
        for ref, coef_at, triples in work:
            coefs = load_coefs(ref, coef_at + row)
            for triple in triples:
                new = step_tile(src[triple], read_at, WEDGE, coefs)
                for v in range(3):
                    dst[triple][pl.ds(wedge_at + v * WEDGE, TILE), :] = new[v]
        if step < STEPS:
            lean(step)

    done = refs[STEPS % 2]
    place = in_strip()
    lanes = lane_ids()
    edge = (lanes < HALO) | (lanes >= LANES - HALO)
    full = members // SLOTS
    for v in range(3):

        def strip(g):
            return done[members + g][pl.ds(wedge_at + v * WEDGE, TILE), :]

        for q in range(full + 1):
            west, east = (strip(q), strip(full + q)) if q < full else (strip(2 * full), rotate(strip(2 * full), -MIX))
            both = jnp.where((place >= HALO) & (place < 2 * HALO), west, east)
            for s in range(min(SLOTS, members - SLOTS * q)):
                m = SLOTS * q + s
                inner = done[m][pl.ds(wedge_at + v * WEDGE, TILE), :]
                fields[m, v] = jnp.where(edge, rotate(both, -STRIP * s - HALO), inner)
    for i in range(members):
        for j in range(i, members):
            at = TILE * pair_place(i, j, members)
            pairs[at : at + TILE, :] = (
                fields[i, 0] * fields[j, 0] + fields[i, 1] * fields[j, 1] + fields[i, 2] * fields[j, 2]
            )
    half = members // 2
    sums = []
    for a in range(members + 1):
        for b in range(half, TILE):
            at = TILE * (TILE * a + b)
            pairs[at : at + TILE, :] = jnp.zeros((TILE, LANES), f32)
        total = pairs[pl.ds(TILE * TILE * a, TILE, stride=TILE), :]
        for s in range(1, TILE):
            total = total + pairs[pl.ds(TILE * TILE * a + s, TILE, stride=TILE), :]
        sums.append(total)
    if is_a:
        for a in range(members + 1):
            result[TILE * a : TILE * a + TILE, :] = sums[a]
    else:
        packed = jnp.zeros((TILE, LANES), f32)
        for a in range(members + 1):
            total = jnp.sum(sums[a] + partial_in[TILE * a : TILE * a + TILE, :], axis=1, keepdims=True)
            packed = jnp.where(lanes == a, total, packed)
        packed = pltpu.roll(packed, 0, axis=1, stride=SPREAD, stride_axis=0)
        result[...] = jnp.broadcast_to(jnp.sum(packed, axis=0, keepdims=True), result.shape)


SPREAD = LANES // TILE


def pair_place(i, j, members):
    b = min(i, members - 1 - i)
    a = j - b if i == b else j + 1
    return TILE * a + b


def first_side_kernel(members, own, halo, facts, hist_c, hist_e, strip_base, fields, result, *scratch):
    side_kernel(members, True, own, halo, facts, hist_c, hist_e, strip_base, None, fields, result, *scratch)


def finish_kernel(members, count, fields_a, fields_b, got, out, factor_out, done, factor, sems):
    total = got[0:TILE, :]
    for r in range(TILE, got.shape[0], TILE):
        total = total + got[r : r + TILE, :]
    packed = jnp.sum(total, axis=0, keepdims=True) / count
    packed = jnp.broadcast_to(packed, (TILE, LANES))
    rows = []
    for i in range(members):
        b = min(i, members - 1 - i)
        rows.append(rotate(packed, b - SPREAD * b if i == b else -1 - SPREAD * b))
    a_at = pl.multiple_of(jnp.where(is_even("lat"), TILE, 0), TILE)
    places = [a_at, pl.multiple_of(TILE - a_at, TILE)]
    x = [[[ref[m, v] for v in range(3)] for ref in (fields_a, fields_b)] for m in range(members)]
    lanes = lane_ids()
    copies = []
    for k in range(members):
        spread = [
            jnp.broadcast_to(rows[k][:, i : i + 1], (TILE, LANES)) if i >= k else None for i in range(members)
        ]
        inverse = 1.0 / spread[k]
        scale = lax.rsqrt(spread[k])
        for half in range(2):
            for v in range(3):
                done[k, v, pl.ds(places[half], TILE), :] = x[k][half][v] * scale
        copy = pltpu.make_async_copy(done.at[k], out.at[k], sems.at[k])
        copy.start()
        copies.append(copy)
        kept = (lanes >= k) & (lanes < members)
        factor[k : k + 1, :] = jnp.where(kept, rows[k] * scale, 0.0)[0:1, :members]
        for i in range(k + 1, members):
            times = spread[i] * inverse
            rows[i] = rows[i] - times * rows[k]
            for half in range(2):
                for v in range(3):
                    x[i][half][v] = x[i][half][v] - times * x[k][half][v]
    copy = pltpu.make_async_copy(factor, factor_out, sems.at[members])
    copy.start()
    for copy in copies + [copy]:
        copy.wait()


def swap(block, axis, count, even_up, periodic):
    pairs = []
    for i in range(count):
        other = i + 1 if (i % 2 == 0) == even_up else i - 1
        if periodic:
            other %= count
        if 0 <= other < count:
            pairs.append((i, other))
    return lax.ppermute(block, axis, pairs)


def shape(*dims):
    return jax.ShapeDtypeStruct(dims, f32)


def cost(flops):
    return pl.CostEstimate(flops=flops, bytes_accessed=1_000_000, transcendentals=0)


def per_device(perturbations, base_wind, base_height):
    members, _, rows, cols = perturbations.shape
    n_lat, n_lon = lax.axis_size("lat"), lax.axis_size("lon")
    total_rows, total_cols = rows * n_lat, cols * n_lon
    groups = len(strip_kinds(members))
    planes_c, planes_e = 3 * members, 3 * groups

    own, msg_a, msg_b = pl.pallas_call(
        functools.partial(load_kernel, members),
        out_shape=[shape(members + 1, 3, rows, LANES), shape(3, rows, LANES), shape(3, rows, LANES)],
        in_specs=[HBM] * 3,
        out_specs=[VMEM] * 3,
        scratch_shapes=[pltpu.SemaphoreType.DMA((6,))],
        compiler_params=PARAMS,
        name="load",
    )(*(pltpu.with_memory_space_constraint(x, pltpu.HBM) for x in (perturbations, base_wind, base_height)))
    got_b = swap(msg_b, "lon", n_lon, False, True)
    got_a = swap(msg_a, "lon", n_lon, True, True)

    facts, hist_c = pl.pallas_call(
        functools.partial(centre_kernel, members, total_rows),
        out_shape=[shape(2, FACTS, LANES), shape(2, STEPS, planes_c, TILE, LANES)],
        in_specs=[VMEM],
        out_specs=[VMEM] * 2,
        scratch_shapes=[
            pltpu.VMEM((FRONT + planes_c * PYRAMID, LANES), f32),
            pltpu.VMEM((FRONT + planes_c * PYRAMID, LANES), f32),
            pltpu.VMEM((FRONT + 3 * PYRAMID, LANES), f32),
            pltpu.VMEM((NCOEF * FACTS, LANES), f32),
        ],
        compiler_params=PARAMS,
        cost_estimate=cost(3_000_000),
        name="centre",
    )(own)

    send = shape(3 * members + 9, TILE, LANES)
    send_a, send_b, west, east = pl.pallas_call(
        functools.partial(meet_kernel, members),
        out_shape=[send, send, shape(3, rows, LANES), shape(3, rows, LANES)],
        in_specs=[VMEM] * 3,
        out_specs=[VMEM] * 4,
        compiler_params=PARAMS,
        name="meet",
    )(own, got_a, got_b)
    halo_a = swap(send_a, "lat", n_lat, True, False)
    halo_b = swap(send_b, "lat", n_lat, False, False)

    hist_e, strip_base = pl.pallas_call(
        functools.partial(edges_kernel, members),
        out_shape=[shape(2, STEPS, planes_e, TILE, LANES), shape(KINDS, 3, rows, LANES)],
        in_specs=[VMEM] * 4,
        out_specs=[VMEM] * 2,
        scratch_shapes=[
            pltpu.VMEM((FRONT + planes_e * PYRAMID, LANES), f32),
            pltpu.VMEM((FRONT + planes_e * PYRAMID, LANES), f32),
            pltpu.VMEM((FRONT + 3 * KINDS * PYRAMID, LANES), f32),
            pltpu.VMEM((KINDS * NCOEF * FACTS, LANES), f32),
        ],
        compiler_params=PARAMS,
        cost_estimate=cost(2_000_000),
        name="edges",
    )(own, west, east, facts)

    wedges = [
        pltpu.VMEM((3 * BASE, LANES), f32),
        pltpu.VMEM((3 * KINDS * BASE, LANES), f32),
        pltpu.VMEM((NCOEF * FACTS, LANES), f32),
        pltpu.VMEM((KINDS * NCOEF * FACTS, LANES), f32),
        pltpu.VMEM((TILE * LANES, LANES), f32),
    ] + [pltpu.VMEM((3 * WEDGE, LANES), f32)] * (2 * (members + groups))
    half = shape(members, 3, TILE, LANES)
    fields_a, partial = pl.pallas_call(
        functools.partial(first_side_kernel, members),
        out_shape=[half, shape((members + 1) * TILE, LANES)],
        in_specs=[VMEM] * 6,
        out_specs=[VMEM] * 2,
        scratch_shapes=wedges,
        compiler_params=PARAMS,
        cost_estimate=cost(4_000_000),
        name="side_a",
    )(own, halo_a, facts, hist_c, hist_e, strip_base)
    fields_b, send_gram = pl.pallas_call(
        functools.partial(side_kernel, members, False),
        out_shape=[half, shape(n_lat * n_lon, LANES)],
        in_specs=[VMEM] * 7,
        out_specs=[VMEM] * 2,
        scratch_shapes=wedges,
        compiler_params=PARAMS,
        cost_estimate=cost(4_000_000),
        name="side_b",
    )(own, halo_b, facts, hist_c, hist_e, strip_base, partial)

    got = lax.all_to_all(send_gram, ("lon", "lat"), 0, 0, tiled=True)

    return pl.pallas_call(
        functools.partial(finish_kernel, members, float(3 * total_rows * total_cols)),
        out_shape=[shape(*perturbations.shape), shape(members, members)],
        in_specs=[VMEM] * 3,
        out_specs=[HBM, HBM],
        scratch_shapes=[
            pltpu.VMEM(perturbations.shape, f32),
            pltpu.VMEM((members, members), f32),
            pltpu.SemaphoreType.DMA((members + 1,)),
        ],
        compiler_params=PARAMS,
        name="finish",
    )(fields_a, fields_b, got)


def solution(mesh):
    return jax.shard_map(
        per_device,
        mesh=mesh,
        in_specs=(P(None, None, "lat", "lon"), P(None, "lat", "lon"), P("lat", "lon")),
        out_specs=(P(None, None, "lat", "lon"), P()),
        check_vma=False,
    )
```

```python
import functools
import math

import jax
import jax.numpy as jnp
from jax import lax
from jax.experimental import pallas as pl
from jax.experimental.pallas import tpu as pltpu
from jax.sharding import PartitionSpec as P

STEPS = 8
HALO = STEPS
TILE = 8
LANES = 128
FACTS = 40
STRIP = 3 * HALO
SLOTS = LANES // STRIP
MIX = 2 * STRIP + HALO
KINDS = 3
NCOEF = 18

advect_rate = 0.1
turn_rate = 0.5
gravity_rate = 0.2
diffuse_rate = 0.12

f32 = jnp.float32
VMEM = pl.BlockSpec(memory_space=pltpu.VMEM)
HBM = pl.BlockSpec(memory_space=pltpu.HBM)
PARAMS = pltpu.CompilerParams(vmem_limit_bytes=40 * 1024 * 1024)


def rotate(x, amount):
    amount = amount % LANES
    return x if amount == 0 else pltpu.roll(x, amount, axis=x.ndim - 1)


def lane_ids(rows=TILE):
    return lax.broadcasted_iota(jnp.int32, (rows, LANES), 1)


def dynamic_zero():
    return jnp.minimum(lax.axis_index("lat"), 0)


def is_even(axis):
    return lax.rem(lax.axis_index(axis), 2) == 0


def store_coefs(base, at, stride, facts, facts_at, coef, coef_at, tiles):
    half = 0.5 * advect_rate
    for t in tiles:
        m = facts[0, pl.ds(facts_at + TILE * t, TILE), :]
        turn = facts[1, pl.ds(facts_at + TILE * t, TILE), :]

        def three(v):
            return [base[pl.ds(at + v * stride + TILE * t + d, TILE), :] for d in range(3)]

        us, u, un = three(0)
        vs, v, vn = three(1)
        hs, h, hn = three(2)
        ue, ve, he = rotate(u, -1), rotate(v, -1), rotate(h, -1)
        uw, vw, hw = rotate(u, 1), rotate(v, 1), rotate(h, 1)
        centre = (1.0 - 4.0 * diffuse_rate) * m
        dif = diffuse_rate * m
        am = half * m
        values = [
            dif - am * u,
            dif + am * u,
            dif - am * v,
            dif + am * v,
            centre - am * (ue - uw),
            turn - am * (un - us),
            centre - am * (vn - vs),
            -turn - am * (ve - vw),
            (0.5 * gravity_rate) * m,
            dif - am * ue,
            dif + am * uw,
            dif - am * vn,
            dif + am * vs,
            -am * he,
            am * hw,
            -am * hn,
            am * hs,
            centre,
        ]
        for i, value in enumerate(values):
            coef[pl.ds(coef_at + i * FACTS + TILE * t, TILE), :] = value


def load_coefs(coef, at):
    return [coef[pl.ds(at + i * FACTS, TILE), :] for i in range(NCOEF)]


def step_tile(src, at, stride, coefs):
    (ae, aw, an, as_, cu, du, cv, dv, k1, he, hw, hn, hs, ue, uw, vn, vs, c0) = coefs

    def three(v):
        return [src[pl.ds(at + v * stride + d, TILE), :] for d in range(3)]

    u_s, u, u_n = three(0)
    v_s, v, v_n = three(1)
    h_s, h, h_n = three(2)
    u_e, v_e, h_e = rotate(u, -1), rotate(v, -1), rotate(h, -1)
    u_w, v_w, h_w = rotate(u, 1), rotate(v, 1), rotate(h, 1)
    new_u = (ae * u_e + aw * u_w) + (an * u_n + as_ * u_s) + (cu * u + du * v) + k1 * (h_w - h_e)
    new_v = (ae * v_e + aw * v_w) + (an * v_n + as_ * v_s) + (cv * v + dv * u) + k1 * (h_s - h_n)
    new_h = (he * h_e + hw * h_w) + (hn * h_n + hs * h_s) + (ue * u_e + uw * u_w) + (vn * v_n + vs * v_s) + c0 * h
    return new_u, new_v, new_h


PYRAMID = 24
FRONT = 8


def pyramid(refs, zero, work, hist):
    def keep(step, source, plane):
        start = zero + FRONT + plane * PYRAMID
        hist[0, step, plane] = source[pl.ds(start, TILE), :]
        hist[1, step, plane] = source[pl.ds(start + TILE - 2 * step, TILE), :]

    for step in range(1, STEPS):
        src, dst = refs[(step - 1) % 2], refs[step % 2]
        for t in range(-(-(16 - 2 * step) // TILE)):
            for coef, coef_at, triples in work:
                coefs = load_coefs(coef, coef_at + TILE * t + step - 1)
                for triple in triples:
                    at = FRONT + 3 * triple * PYRAMID + TILE * t
                    new = step_tile(src, zero + at, PYRAMID, coefs)
                    for v in range(3):
                        dst[pl.ds(zero + at + v * PYRAMID, TILE), :] = new[v]
        for _, _, triples in work:
            for triple in triples:
                for v in range(3):
                    keep(step, dst, 3 * triple + v)


def first_level(hist, plane, low, high):
    hist[0, 0, plane] = low
    hist[1, 0, plane] = high


def slot_range(s, shift):
    lanes = (lane_ids() + shift) % LANES
    return (lanes >= STRIP * s) & (lanes < STRIP * s + STRIP)


def in_strip():
    return lane_ids() % STRIP


def own_strips(rows_of, members):
    vectors = []
    for q in range(-(-members // SLOTS)):
        west = east = None
        for s in range(min(SLOTS, members - SLOTS * q)):
            moved = rotate(rows_of(SLOTS * q + s), STRIP * s + HALO)
            west = moved if s == 0 else jnp.where(slot_range(s, 0), moved, west)
            east = moved if s == 0 else jnp.where(slot_range(s, HALO), moved, east)
        vectors.append((west, east))
    return vectors


def base_own_strips(rows):
    west = east = None
    for s in range(SLOTS):
        moved = rotate(rows, STRIP * s + HALO)
        west = moved if s == 0 else jnp.where(slot_range(s, 0), moved, west)
        east = moved if s == 0 else jnp.where(slot_range(s, HALO), moved, east)
    return west, east


def mix(west, east):
    return jnp.where(lane_ids() < 2 * STRIP, west, rotate(east, MIX))


def fill_strips(vectors, west_halo, east_halo):
    place = in_strip()
    wests, easts = [], []
    for q, (west, east) in enumerate(vectors):
        wests.append(jnp.where(place < HALO, rotate(west_halo, -HALO * q), west))
        here = (place >= HALO) & (place < 2 * HALO)
        easts.append(jnp.where(here, rotate(east_halo, -HALO * q), east))
    return wests[:-1] + easts[:-1] + [mix(wests[-1], easts[-1])]


def base_strips(rows, west_halo, east_halo, members):
    q, first = members // SLOTS, members % SLOTS
    place = in_strip()
    west, east = base_own_strips(rows)

    def everywhere(halo, edge):
        near = rotate(halo, -HALO * q)
        return jnp.where(lane_ids() < STRIP * first + edge, rotate(near, -STRIP * first), near)

    west = jnp.where(place < HALO, everywhere(west_halo, 0), west)
    here = (place >= HALO) & (place < 2 * HALO)
    east = jnp.where(here, everywhere(east_halo, HALO), east)
    return west, east, mix(west, east)


def strip_kinds(members):
    full = members // SLOTS
    return [0] * full + [1] * full + [2]


def load_kernel(members, pert, wind, height, own, msg_a, msg_b, sems):
    chunk = members // 4
    copies = [
        pltpu.make_async_copy(wind, own.at[members, pl.ds(0, 2)], sems.at[0]),
        pltpu.make_async_copy(height, own.at[members, 2], sems.at[1]),
    ]
    for i in range(4):
        part = pl.ds(i * chunk, chunk)
        copies.append(pltpu.make_async_copy(pert.at[part], own.at[part], sems.at[2 + i]))
    for copy in copies:
        copy.start()
    for copy in copies:
        copy.wait()
    lon_even = is_even("lon")
    lanes = lane_ids()
    for v in range(3):
        for t in range(2):
            rows = slice(TILE * t, TILE * t + TILE)
            to_e = to_w = None
            for q in range(3):
                for s in range(SLOTS):
                    low = STRIP * s + HALO * q
                    moved = rotate(own[min(SLOTS * q + s, members), v, rows, :], low + HALO)
                    if to_e is None:
                        to_e = to_w = moved
                    else:
                        to_e = jnp.where((lanes >= low) & (lanes < low + HALO), moved, to_e)
                        to_w = jnp.where((lanes >= low + HALO) & (lanes < low + 2 * HALO), moved, to_w)
            msg_a[v, rows, :] = jnp.where(lon_even, to_e, to_w)
            msg_b[v, rows, :] = jnp.where(lon_even, to_w, to_e)


def centre_kernel(members, total_rows, own, msg, facts, hist, msg_late, first, second, base, coef):
    msg_late[...] = msg[...]
    zero = dynamic_zero()
    start = lax.axis_index("lat") * 16 - HALO + 1
    for t in range(FACTS // TILE):
        glob = start + TILE * t + lax.broadcasted_iota(jnp.int32, (TILE, LANES), 0)
        inside = ((glob >= 0) & (glob < total_rows)).astype(f32)
        rows = slice(TILE * t, TILE * t + TILE)
        facts[0, rows, :] = inside
        facts[1, rows, :] = turn_rate * inside * jnp.sin(math.pi * ((glob.astype(f32) + 0.5) / total_rows - 0.5))
    for m in range(members + 1):
        for v in range(3):
            low, high = own[m, v, 0:TILE, :], own[m, v, TILE:16, :]
            plane = 3 * m + v
            if m < members:
                ref, at = first, FRONT + plane * PYRAMID
                first_level(hist, plane, low, high)
            else:
                ref, at = base, FRONT + v * PYRAMID
            ref[at : at + TILE, :] = low
            ref[at + TILE : at + 16, :] = high
    store_coefs(base, zero + FRONT, PYRAMID, facts, HALO, coef, zero, range(2))
    pyramid([first, second], zero, [(coef, zero, list(range(members)))], hist)


def meet_kernel(members, own, got_a, got_b, send_a, send_b, west, east):
    lat_even, lon_even = is_even("lat"), is_even("lon")
    low = pl.multiple_of(jnp.where(lat_even, TILE, 0), TILE)
    for send, at in ((send_a, low), (send_b, TILE - low)):
        at = pl.multiple_of(at, TILE)
        for m in range(members + 1):
            for v in range(3):
                send[3 * m + v] = own[m, v, pl.ds(at, TILE), :]
        for v in range(3):
            a, b = got_a[v, pl.ds(at, TILE), :], got_b[v, pl.ds(at, TILE), :]
            send[3 * members + 3 + v] = jnp.where(lon_even, b, a)
            send[3 * members + 6 + v] = jnp.where(lon_even, a, b)
    for v in range(3):
        for t in range(2):
            rows = slice(TILE * t, TILE * t + TILE)
            west[v, rows, :] = jnp.where(lon_even, got_b[v, rows, :], got_a[v, rows, :])
            east[v, rows, :] = jnp.where(lon_even, got_a[v, rows, :], got_b[v, rows, :])


def edges_kernel(members, own, west, east, facts, hist, strip_base, first, second, base, coef):
    zero = dynamic_zero()
    kinds = strip_kinds(members)
    for v in range(3):
        for t in range(2):
            rows = slice(TILE * t, TILE * t + TILE)
            halos = west[v, rows, :], east[v, rows, :]
            strips = fill_strips(own_strips(lambda m: own[m, v, rows, :], members), *halos)
            for g, strip in enumerate(strips):
                at = FRONT + (3 * g + v) * PYRAMID + TILE * t
                first[at : at + TILE, :] = strip
                hist[t, 0, 3 * g + v] = strip
            for kind, strip in enumerate(base_strips(own[members, v, rows, :], *halos, members)):
                at = FRONT + (3 * kind + v) * PYRAMID + TILE * t
                base[at : at + TILE, :] = strip
                strip_base[kind, v, rows, :] = strip
    work = []
    for kind in range(KINDS):
        coef_at = zero + kind * NCOEF * FACTS
        store_coefs(base, zero + FRONT + 3 * kind * PYRAMID, PYRAMID, facts, HALO, coef, coef_at, range(2))
        work.append((coef, coef_at, [g for g in range(len(kinds)) if kinds[g] == kind]))
    pyramid([first, second], zero, work, hist)


WEDGE = 16
BASE = 40


def side_kernel(
    members, is_a, own, halo, facts, hist_c, hist_e, strip_base, partial_in, fields, result, *scratch
):
    base, base_e, coef, coef_e, pairs = scratch[:5]
    count = (len(scratch) - 5) // 2
    first, second = scratch[5 : 5 + count], scratch[5 + count :]
    north = jnp.logical_not(is_even("lat")) if is_a else is_even("lat")
    side = jnp.where(north, 0, 1)
    wedge_at = jnp.where(north, 0, TILE)
    hist_at = jnp.where(north, TILE, 0)
    read_at = jnp.where(north, 0, TILE - 2)
    own_at = jnp.where(north, 2 * TILE, 1)
    halo_at = jnp.where(north, TILE, 2 * TILE + 1)
    facts_at = jnp.where(north, 0, 2 * TILE - 1)
    zero = dynamic_zero()
    kinds = strip_kinds(members)
    groups = len(kinds)
    triples_c = list(range(members))
    planes_c = 3 * members

    for m in range(members):
        for v in range(3):
            first[m][pl.ds(wedge_at + v * WEDGE, TILE), :] = halo[3 * m + v]
    for v in range(3):
        west, east = halo[planes_c + 3 + v], halo[planes_c + 6 + v]
        strips = fill_strips(own_strips(lambda m: halo[3 * m + v], members), west, east)
        for g, strip in enumerate(strips):
            first[members + g][pl.ds(wedge_at + v * WEDGE, TILE), :] = strip
        for t in range(2):
            base[pl.ds(own_at + v * BASE + TILE * t, TILE), :] = own[members, v, TILE * t : TILE * t + TILE, :]
        base[pl.ds(halo_at + v * BASE, TILE), :] = halo[planes_c + v]
        for kind, strip in enumerate(base_strips(halo[planes_c + v], west, east, members)):
            plane = 3 * kind + v
            for t in range(2):
                base_e[pl.ds(own_at + plane * BASE + TILE * t, TILE), :] = strip_base[
                    kind, v, TILE * t : TILE * t + TILE, :
                ]
            base_e[pl.ds(halo_at + plane * BASE, TILE), :] = strip
    store_coefs(base, zero + TILE, BASE, facts, facts_at, coef, zero, range(2))
    work = [(coef, zero, triples_c)]
    for kind in range(KINDS):
        coef_at = zero + kind * NCOEF * FACTS
        store_coefs(base_e, zero + TILE + 3 * kind * BASE, BASE, facts, facts_at, coef_e, coef_at, range(2))
        work.append((coef_e, coef_at, [members + g for g in range(groups) if kinds[g] == kind]))

    refs = [first, second]

    def lean(step):
        for triple, ref in enumerate(refs[step % 2]):
            for v in range(3):
                if triple < members:
                    rows = hist_c[side, step, 3 * triple + v]
                else:
                    rows = hist_e[side, step, 3 * (triple - members) + v]
                ref[pl.ds(hist_at + v * WEDGE, TILE), :] = rows

    lean(0)
    for step in range(1, STEPS + 1):
        src, dst = refs[(step - 1) % 2], refs[step % 2]
        row = jnp.where(north, step - 1, STEPS - step)
        for ref, coef_at, triples in work:
            coefs = load_coefs(ref, coef_at + row)
            for triple in triples:
                new = step_tile(src[triple], read_at, WEDGE, coefs)
                for v in range(3):
                    dst[triple][pl.ds(wedge_at + v * WEDGE, TILE), :] = new[v]
        if step < STEPS:
            lean(step)

    done = refs[STEPS % 2]
    place = in_strip()
    lanes = lane_ids()
    edge = (lanes < HALO) | (lanes >= LANES - HALO)
    full = members // SLOTS
    for v in range(3):

        def strip(g):
            return done[members + g][pl.ds(wedge_at + v * WEDGE, TILE), :]

        for q in range(full + 1):
            west, east = (strip(q), strip(full + q)) if q < full else (strip(2 * full), rotate(strip(2 * full), -MIX))
            both = jnp.where((place >= HALO) & (place < 2 * HALO), west, east)
            for s in range(min(SLOTS, members - SLOTS * q)):
                m = SLOTS * q + s
                inner = done[m][pl.ds(wedge_at + v * WEDGE, TILE), :]
                fields[m, v] = jnp.where(edge, rotate(both, -STRIP * s - HALO), inner)
    for i in range(members):
        for j in range(i, members):
            at = TILE * pair_place(i, j, members)
            pairs[at : at + TILE, :] = (
                fields[i, 0] * fields[j, 0] + fields[i, 1] * fields[j, 1] + fields[i, 2] * fields[j, 2]
            )
    half = members // 2
    sums = []
    for a in range(members + 1):
        for b in range(half, TILE):
            at = TILE * (TILE * a + b)
            pairs[at : at + TILE, :] = jnp.zeros((TILE, LANES), f32)
        total = pairs[pl.ds(TILE * TILE * a, TILE, stride=TILE), :]
        for s in range(1, TILE):
            total = total + pairs[pl.ds(TILE * TILE * a + s, TILE, stride=TILE), :]
        sums.append(total)
    if is_a:
        for a in range(members + 1):
            result[TILE * a : TILE * a + TILE, :] = sums[a]
    else:
        packed = jnp.zeros((TILE, LANES), f32)
        for a in range(members + 1):
            total = jnp.sum(sums[a] + partial_in[TILE * a : TILE * a + TILE, :], axis=1, keepdims=True)
            packed = jnp.where(lanes == a, total, packed)
        packed = pltpu.roll(packed, 0, axis=1, stride=SPREAD, stride_axis=0)
        result[...] = jnp.broadcast_to(jnp.sum(packed, axis=0, keepdims=True), result.shape)


SPREAD = LANES // TILE


def pair_place(i, j, members):
    b = min(i, members - 1 - i)
    a = j - b if i == b else j + 1
    return TILE * a + b


def first_side_kernel(members, own, halo, facts, hist_c, hist_e, strip_base, fields, result, *scratch):
    side_kernel(members, True, own, halo, facts, hist_c, hist_e, strip_base, None, fields, result, *scratch)


def finish_kernel(members, count, fields_a, fields_b, got, out, factor_out, done, factor, sems):
    total = got[0:TILE, :]
    for r in range(TILE, got.shape[0], TILE):
        total = total + got[r : r + TILE, :]
    packed = jnp.sum(total, axis=0, keepdims=True) / count
    packed = jnp.broadcast_to(packed, (TILE, LANES))
    gram = {}
    for i in range(members):
        for j in range(i, members):
            place = pair_place(i, j, members)
            lane = SPREAD * (place % TILE) + place // TILE
            gram[i, j] = jnp.broadcast_to(packed[:, lane : lane + 1], (TILE, LANES))
    a_at = pl.multiple_of(jnp.where(is_even("lat"), TILE, 0), TILE)
    places = [a_at, pl.multiple_of(TILE - a_at, TILE)]
    x = [[[ref[m, v] for v in range(3)] for ref in (fields_a, fields_b)] for m in range(members)]
    lanes = lane_ids()
    copies = []
    for k in range(members):
        scale = lax.rsqrt(gram[k, k])
        for half in range(2):
            for v in range(3):
                x[k][half][v] = x[k][half][v] * scale
                done[k, v, pl.ds(places[half], TILE), :] = x[k][half][v]
        copy = pltpu.make_async_copy(done.at[k], out.at[k], sems.at[k])
        copy.start()
        copies.append(copy)
        row = jnp.zeros((TILE, LANES), f32)
        for i in range(k, members):
            gram[k, i] = gram[k, i] * scale
            row = jnp.where(lanes == i, gram[k, i], row)
        factor[k : k + 1, :] = row[0:1, :members]
        for i in range(k + 1, members):
            for j in range(i, members):
                gram[i, j] = gram[i, j] - gram[k, i] * gram[k, j]
            for half in range(2):
                for v in range(3):
                    x[i][half][v] = x[i][half][v] - gram[k, i] * x[k][half][v]
    copy = pltpu.make_async_copy(factor, factor_out, sems.at[members])
    copy.start()
    for copy in copies + [copy]:
        copy.wait()


def swap(block, axis, count, even_up, periodic):
    pairs = []
    for i in range(count):
        other = i + 1 if (i % 2 == 0) == even_up else i - 1
        if periodic:
            other %= count
        if 0 <= other < count:
            pairs.append((i, other))
    return lax.ppermute(block, axis, pairs)


def shape(*dims):
    return jax.ShapeDtypeStruct(dims, f32)


def cost(flops):
    return pl.CostEstimate(flops=flops, bytes_accessed=1_000_000, transcendentals=0)


def per_device(perturbations, base_wind, base_height):
    members, _, rows, cols = perturbations.shape
    n_lat, n_lon = lax.axis_size("lat"), lax.axis_size("lon")
    total_rows, total_cols = rows * n_lat, cols * n_lon
    groups = len(strip_kinds(members))
    planes_c, planes_e = 3 * members, 3 * groups

    own, msg_a, msg_b = pl.pallas_call(
        functools.partial(load_kernel, members),
        out_shape=[shape(members + 1, 3, rows, LANES), shape(3, rows, LANES), shape(3, rows, LANES)],
        in_specs=[HBM] * 3,
        out_specs=[VMEM] * 3,
        scratch_shapes=[pltpu.SemaphoreType.DMA((6,))],
        compiler_params=PARAMS,
        name="load",
    )(*(pltpu.with_memory_space_constraint(x, pltpu.HBM) for x in (perturbations, base_wind, base_height)))
    got_b = swap(msg_b, "lon", n_lon, False, True)

    facts, hist_c, msg_a = pl.pallas_call(
        functools.partial(centre_kernel, members, total_rows),
        out_shape=[shape(2, FACTS, LANES), shape(2, STEPS, planes_c, TILE, LANES), shape(3, rows, LANES)],
        in_specs=[VMEM] * 2,
        out_specs=[VMEM] * 3,
        scratch_shapes=[
            pltpu.VMEM((FRONT + planes_c * PYRAMID, LANES), f32),
            pltpu.VMEM((FRONT + planes_c * PYRAMID, LANES), f32),
            pltpu.VMEM((FRONT + 3 * PYRAMID, LANES), f32),
            pltpu.VMEM((NCOEF * FACTS, LANES), f32),
        ],
        compiler_params=PARAMS,
        cost_estimate=cost(3_000_000),
        name="centre",
    )(own, msg_a)
    got_a = swap(msg_a, "lon", n_lon, True, True)

    send = shape(3 * members + 9, TILE, LANES)
    send_a, send_b, west, east = pl.pallas_call(
        functools.partial(meet_kernel, members),
        out_shape=[send, send, shape(3, rows, LANES), shape(3, rows, LANES)],
        in_specs=[VMEM] * 3,
        out_specs=[VMEM] * 4,
        compiler_params=PARAMS,
        name="meet",
    )(own, got_a, got_b)
    halo_a = swap(send_a, "lat", n_lat, True, False)
    halo_b = swap(send_b, "lat", n_lat, False, False)

    hist_e, strip_base = pl.pallas_call(
        functools.partial(edges_kernel, members),
        out_shape=[shape(2, STEPS, planes_e, TILE, LANES), shape(KINDS, 3, rows, LANES)],
        in_specs=[VMEM] * 4,
        out_specs=[VMEM] * 2,
        scratch_shapes=[
            pltpu.VMEM((FRONT + planes_e * PYRAMID, LANES), f32),
            pltpu.VMEM((FRONT + planes_e * PYRAMID, LANES), f32),
            pltpu.VMEM((FRONT + 3 * KINDS * PYRAMID, LANES), f32),
            pltpu.VMEM((KINDS * NCOEF * FACTS, LANES), f32),
        ],
        compiler_params=PARAMS,
        cost_estimate=cost(2_000_000),
        name="edges",
    )(own, west, east, facts)

    wedges = [
        pltpu.VMEM((3 * BASE, LANES), f32),
        pltpu.VMEM((3 * KINDS * BASE, LANES), f32),
        pltpu.VMEM((NCOEF * FACTS, LANES), f32),
        pltpu.VMEM((KINDS * NCOEF * FACTS, LANES), f32),
        pltpu.VMEM((TILE * LANES, LANES), f32),
    ] + [pltpu.VMEM((3 * WEDGE, LANES), f32)] * (2 * (members + groups))
    half = shape(members, 3, TILE, LANES)
    fields_a, partial = pl.pallas_call(
        functools.partial(first_side_kernel, members),
        out_shape=[half, shape((members + 1) * TILE, LANES)],
        in_specs=[VMEM] * 6,
        out_specs=[VMEM] * 2,
        scratch_shapes=wedges,
        compiler_params=PARAMS,
        cost_estimate=cost(4_000_000),
        name="side_a",
    )(own, halo_a, facts, hist_c, hist_e, strip_base)
    fields_b, send_gram = pl.pallas_call(
        functools.partial(side_kernel, members, False),
        out_shape=[half, shape(n_lat * n_lon, LANES)],
        in_specs=[VMEM] * 7,
        out_specs=[VMEM] * 2,
        scratch_shapes=wedges,
        compiler_params=PARAMS,
        cost_estimate=cost(4_000_000),
        name="side_b",
    )(own, halo_b, facts, hist_c, hist_e, strip_base, partial)

    got = lax.all_to_all(send_gram, ("lon", "lat"), 0, 0, tiled=True)

    return pl.pallas_call(
        functools.partial(finish_kernel, members, float(3 * total_rows * total_cols)),
        out_shape=[shape(*perturbations.shape), shape(members, members)],
        in_specs=[VMEM] * 3,
        out_specs=[HBM, HBM],
        scratch_shapes=[
            pltpu.VMEM(perturbations.shape, f32),
            pltpu.VMEM((members, members), f32),
            pltpu.SemaphoreType.DMA((members + 1,)),
        ],
        compiler_params=PARAMS,
        name="finish",
    )(fields_a, fields_b, got)


def solution(mesh):
    return jax.shard_map(
        per_device,
        mesh=mesh,
        in_specs=(P(None, None, "lat", "lon"), P(None, "lat", "lon"), P("lat", "lon")),
        out_specs=(P(None, None, "lat", "lon"), P()),
        check_vma=False,
    )
```

```python
import functools
import math

import jax
import jax.numpy as jnp
from jax import lax
from jax.experimental import pallas as pl
from jax.experimental.pallas import tpu as pltpu
from jax.sharding import PartitionSpec as P

STEPS = 8
HALO = STEPS
TILE = 8
LANES = 128
FACTS = 40
STRIP = 3 * HALO
SLOTS = LANES // STRIP
MIX = 2 * STRIP + HALO
KINDS = 3
NCOEF = 18

advect_rate = 0.1
turn_rate = 0.5
gravity_rate = 0.2
diffuse_rate = 0.12

f32 = jnp.float32
VMEM = pl.BlockSpec(memory_space=pltpu.VMEM)
HBM = pl.BlockSpec(memory_space=pltpu.HBM)
PARAMS = pltpu.CompilerParams(vmem_limit_bytes=40 * 1024 * 1024)


def rotate(x, amount):
    amount = amount % LANES
    return x if amount == 0 else pltpu.roll(x, amount, axis=x.ndim - 1)


def lane_ids(rows=TILE):
    return lax.broadcasted_iota(jnp.int32, (rows, LANES), 1)


def dynamic_zero():
    return jnp.minimum(lax.axis_index("lat"), 0)


def is_even(axis):
    return lax.rem(lax.axis_index(axis), 2) == 0


def store_coefs(base, at, stride, facts, facts_at, coef, coef_at, tiles):
    half = 0.5 * advect_rate
    for t in tiles:
        m = facts[0, pl.ds(facts_at + TILE * t, TILE), :]
        turn = facts[1, pl.ds(facts_at + TILE * t, TILE), :]

        def three(v):
            return [base[pl.ds(at + v * stride + TILE * t + d, TILE), :] for d in range(3)]

        us, u, un = three(0)
        vs, v, vn = three(1)
        hs, h, hn = three(2)
        ue, ve, he = rotate(u, -1), rotate(v, -1), rotate(h, -1)
        uw, vw, hw = rotate(u, 1), rotate(v, 1), rotate(h, 1)
        centre = (1.0 - 4.0 * diffuse_rate) * m
        dif = diffuse_rate * m
        am = half * m
        values = [
            dif - am * u,
            dif + am * u,
            dif - am * v,
            dif + am * v,
            centre - am * (ue - uw),
            turn - am * (un - us),
            centre - am * (vn - vs),
            -turn - am * (ve - vw),
            (0.5 * gravity_rate) * m,
            dif - am * ue,
            dif + am * uw,
            dif - am * vn,
            dif + am * vs,
            -am * he,
            am * hw,
            -am * hn,
            am * hs,
            centre,
        ]
        for i, value in enumerate(values):
            coef[pl.ds(coef_at + i * FACTS + TILE * t, TILE), :] = value


def load_coefs(coef, at):
    return [coef[pl.ds(at + i * FACTS, TILE), :] for i in range(NCOEF)]


def step_tile(src, at, stride, coefs):
    (ae, aw, an, as_, cu, du, cv, dv, k1, he, hw, hn, hs, ue, uw, vn, vs, c0) = coefs

    def three(v):
        return [src[pl.ds(at + v * stride + d, TILE), :] for d in range(3)]

    u_s, u, u_n = three(0)
    v_s, v, v_n = three(1)
    h_s, h, h_n = three(2)
    u_e, v_e, h_e = rotate(u, -1), rotate(v, -1), rotate(h, -1)
    u_w, v_w, h_w = rotate(u, 1), rotate(v, 1), rotate(h, 1)
    new_u = (ae * u_e + aw * u_w) + (an * u_n + as_ * u_s) + (cu * u + du * v) + k1 * (h_w - h_e)
    new_v = (ae * v_e + aw * v_w) + (an * v_n + as_ * v_s) + (cv * v + dv * u) + k1 * (h_s - h_n)
    new_h = (he * h_e + hw * h_w) + (hn * h_n + hs * h_s) + (ue * u_e + uw * u_w) + (vn * v_n + vs * v_s) + c0 * h
    return new_u, new_v, new_h


PYRAMID = 24
FRONT = 8


def pyramid(refs, zero, work, hist):
    def keep(step, source, plane):
        start = zero + FRONT + plane * PYRAMID
        hist[0, step, plane] = source[pl.ds(start, TILE), :]
        hist[1, step, plane] = source[pl.ds(start + TILE - 2 * step, TILE), :]

    for step in range(1, STEPS):
        src, dst = refs[(step - 1) % 2], refs[step % 2]
        for t in range(-(-(16 - 2 * step) // TILE)):
            for coef, coef_at, triples in work:
                coefs = load_coefs(coef, coef_at + TILE * t + step - 1)
                for triple in triples:
                    at = FRONT + 3 * triple * PYRAMID + TILE * t
                    new = step_tile(src, zero + at, PYRAMID, coefs)
                    for v in range(3):
                        dst[pl.ds(zero + at + v * PYRAMID, TILE), :] = new[v]
        for _, _, triples in work:
            for triple in triples:
                for v in range(3):
                    keep(step, dst, 3 * triple + v)


def first_level(hist, plane, low, high):
    hist[0, 0, plane] = low
    hist[1, 0, plane] = high


def slot_range(s, shift):
    lanes = (lane_ids() + shift) % LANES
    return (lanes >= STRIP * s) & (lanes < STRIP * s + STRIP)


def in_strip():
    return lane_ids() % STRIP


def own_strips(rows_of, members):
    vectors = []
    for q in range(-(-members // SLOTS)):
        west = east = None
        for s in range(min(SLOTS, members - SLOTS * q)):
            moved = rotate(rows_of(SLOTS * q + s), STRIP * s + HALO)
            west = moved if s == 0 else jnp.where(slot_range(s, 0), moved, west)
            east = moved if s == 0 else jnp.where(slot_range(s, HALO), moved, east)
        vectors.append((west, east))
    return vectors


def base_own_strips(rows):
    west = east = None
    for s in range(SLOTS):
        moved = rotate(rows, STRIP * s + HALO)
        west = moved if s == 0 else jnp.where(slot_range(s, 0), moved, west)
        east = moved if s == 0 else jnp.where(slot_range(s, HALO), moved, east)
    return west, east


def mix(west, east):
    return jnp.where(lane_ids() < 2 * STRIP, west, rotate(east, MIX))


def fill_strips(vectors, west_halo, east_halo):
    place = in_strip()
    wests, easts = [], []
    for q, (west, east) in enumerate(vectors):
        wests.append(jnp.where(place < HALO, rotate(west_halo, -HALO * q), west))
        here = (place >= HALO) & (place < 2 * HALO)
        easts.append(jnp.where(here, rotate(east_halo, -HALO * q), east))
    return wests[:-1] + easts[:-1] + [mix(wests[-1], easts[-1])]


def base_strips(rows, west_halo, east_halo, members):
    q, first = members // SLOTS, members % SLOTS
    place = in_strip()
    west, east = base_own_strips(rows)

    def everywhere(halo, edge):
        near = rotate(halo, -HALO * q)
        return jnp.where(lane_ids() < STRIP * first + edge, rotate(near, -STRIP * first), near)

    west = jnp.where(place < HALO, everywhere(west_halo, 0), west)
    here = (place >= HALO) & (place < 2 * HALO)
    east = jnp.where(here, everywhere(east_halo, HALO), east)
    return west, east, mix(west, east)


def strip_kinds(members):
    full = members // SLOTS
    return [0] * full + [1] * full + [2]


def load_kernel(members, pert, wind, height, own, msg_a, msg_b, sems):
    chunk = members // 4
    copies = [
        pltpu.make_async_copy(wind, own.at[members, pl.ds(0, 2)], sems.at[0]),
        pltpu.make_async_copy(height, own.at[members, 2], sems.at[1]),
    ]
    for i in range(4):
        part = pl.ds(i * chunk, chunk)
        copies.append(pltpu.make_async_copy(pert.at[part], own.at[part], sems.at[2 + i]))
    for copy in copies:
        copy.start()
    for copy in copies:
        copy.wait()
    lon_even = is_even("lon")
    lanes = lane_ids()
    for v in range(3):
        for t in range(2):
            rows = slice(TILE * t, TILE * t + TILE)
            to_e = to_w = None
            for q in range(3):
                for s in range(SLOTS):
                    low = STRIP * s + HALO * q
                    moved = rotate(own[min(SLOTS * q + s, members), v, rows, :], low + HALO)
                    if to_e is None:
                        to_e = to_w = moved
                    else:
                        to_e = jnp.where((lanes >= low) & (lanes < low + HALO), moved, to_e)
                        to_w = jnp.where((lanes >= low + HALO) & (lanes < low + 2 * HALO), moved, to_w)
            msg_a[v, rows, :] = jnp.where(lon_even, to_e, to_w)
            msg_b[v, rows, :] = jnp.where(lon_even, to_w, to_e)


def centre_kernel(members, total_rows, own, facts, hist, first, second, base, coef):
    zero = dynamic_zero()
    start = lax.axis_index("lat") * 16 - HALO + 1
    for t in range(FACTS // TILE):
        glob = start + TILE * t + lax.broadcasted_iota(jnp.int32, (TILE, LANES), 0)
        inside = ((glob >= 0) & (glob < total_rows)).astype(f32)
        rows = slice(TILE * t, TILE * t + TILE)
        facts[0, rows, :] = inside
        facts[1, rows, :] = turn_rate * inside * jnp.sin(math.pi * ((glob.astype(f32) + 0.5) / total_rows - 0.5))
    for m in range(members + 1):
        for v in range(3):
            low, high = own[m, v, 0:TILE, :], own[m, v, TILE:16, :]
            plane = 3 * m + v
            if m < members:
                ref, at = first, FRONT + plane * PYRAMID
                first_level(hist, plane, low, high)
            else:
                ref, at = base, FRONT + v * PYRAMID
            ref[at : at + TILE, :] = low
            ref[at + TILE : at + 16, :] = high
    store_coefs(base, zero + FRONT, PYRAMID, facts, HALO, coef, zero, range(2))
    pyramid([first, second], zero, [(coef, zero, list(range(members)))], hist)


def meet_kernel(members, own, got_b, got_a, facts, send_a, send_b, west, east):
    lat_even, lon_even = is_even("lat"), is_even("lon")
    low = pl.multiple_of(jnp.where(lat_even, TILE, 0), TILE)
    for send, at in ((send_a, low), (send_b, TILE - low)):
        at = pl.multiple_of(at, TILE)
        for m in range(members + 1):
            for v in range(3):
                send[3 * m + v] = own[m, v, pl.ds(at, TILE), :]
        for v in range(3):
            a, b = got_a[v, pl.ds(at, TILE), :], got_b[v, pl.ds(at, TILE), :]
            send[3 * members + 3 + v] = jnp.where(lon_even, b, a)
            send[3 * members + 6 + v] = jnp.where(lon_even, a, b)
    for v in range(3):
        for t in range(2):
            rows = slice(TILE * t, TILE * t + TILE)
            west[v, rows, :] = jnp.where(lon_even, got_b[v, rows, :], got_a[v, rows, :])
            east[v, rows, :] = jnp.where(lon_even, got_a[v, rows, :], got_b[v, rows, :])


def edges_kernel(members, own, west, east, facts, hist, strip_base, first, second, base, coef):
    zero = dynamic_zero()
    kinds = strip_kinds(members)
    for v in range(3):
        for t in range(2):
            rows = slice(TILE * t, TILE * t + TILE)
            halos = west[v, rows, :], east[v, rows, :]
            strips = fill_strips(own_strips(lambda m: own[m, v, rows, :], members), *halos)
            for g, strip in enumerate(strips):
                at = FRONT + (3 * g + v) * PYRAMID + TILE * t
                first[at : at + TILE, :] = strip
                hist[t, 0, 3 * g + v] = strip
            for kind, strip in enumerate(base_strips(own[members, v, rows, :], *halos, members)):
                at = FRONT + (3 * kind + v) * PYRAMID + TILE * t
                base[at : at + TILE, :] = strip
                strip_base[kind, v, rows, :] = strip
    work = []
    for kind in range(KINDS):
        coef_at = zero + kind * NCOEF * FACTS
        store_coefs(base, zero + FRONT + 3 * kind * PYRAMID, PYRAMID, facts, HALO, coef, coef_at, range(2))
        work.append((coef, coef_at, [g for g in range(len(kinds)) if kinds[g] == kind]))
    pyramid([first, second], zero, work, hist)


WEDGE = 16
BASE = 40


def side_kernel(
    members, is_a, own, halo, facts, hist_c, hist_e, strip_base, partial_in, fields, result, *scratch
):
    base, base_e, coef, coef_e, pairs = scratch[:5]
    count = (len(scratch) - 5) // 2
    first, second = scratch[5 : 5 + count], scratch[5 + count :]
    north = jnp.logical_not(is_even("lat")) if is_a else is_even("lat")
    side = jnp.where(north, 0, 1)
    wedge_at = jnp.where(north, 0, TILE)
    hist_at = jnp.where(north, TILE, 0)
    read_at = jnp.where(north, 0, TILE - 2)
    own_at = jnp.where(north, 2 * TILE, 1)
    halo_at = jnp.where(north, TILE, 2 * TILE + 1)
    facts_at = jnp.where(north, 0, 2 * TILE - 1)
    zero = dynamic_zero()
    kinds = strip_kinds(members)
    groups = len(kinds)
    triples_c = list(range(members))
    planes_c = 3 * members

    for m in range(members):
        for v in range(3):
            first[m][pl.ds(wedge_at + v * WEDGE, TILE), :] = halo[3 * m + v]
    for v in range(3):
        west, east = halo[planes_c + 3 + v], halo[planes_c + 6 + v]
        strips = fill_strips(own_strips(lambda m: halo[3 * m + v], members), west, east)
        for g, strip in enumerate(strips):
            first[members + g][pl.ds(wedge_at + v * WEDGE, TILE), :] = strip
        for t in range(2):
            base[pl.ds(own_at + v * BASE + TILE * t, TILE), :] = own[members, v, TILE * t : TILE * t + TILE, :]
        base[pl.ds(halo_at + v * BASE, TILE), :] = halo[planes_c + v]
        for kind, strip in enumerate(base_strips(halo[planes_c + v], west, east, members)):
            plane = 3 * kind + v
            for t in range(2):
                base_e[pl.ds(own_at + plane * BASE + TILE * t, TILE), :] = strip_base[
                    kind, v, TILE * t : TILE * t + TILE, :
                ]
            base_e[pl.ds(halo_at + plane * BASE, TILE), :] = strip
    store_coefs(base, zero + TILE, BASE, facts, facts_at, coef, zero, range(2))
    work = [(coef, zero, triples_c)]
    for kind in range(KINDS):
        coef_at = zero + kind * NCOEF * FACTS
        store_coefs(base_e, zero + TILE + 3 * kind * BASE, BASE, facts, facts_at, coef_e, coef_at, range(2))
        work.append((coef_e, coef_at, [members + g for g in range(groups) if kinds[g] == kind]))

    refs = [first, second]

    def lean(step):
        for triple, ref in enumerate(refs[step % 2]):
            for v in range(3):
                if triple < members:
                    rows = hist_c[side, step, 3 * triple + v]
                else:
                    rows = hist_e[side, step, 3 * (triple - members) + v]
                ref[pl.ds(hist_at + v * WEDGE, TILE), :] = rows

    lean(0)
    for step in range(1, STEPS + 1):
        src, dst = refs[(step - 1) % 2], refs[step % 2]
        row = jnp.where(north, step - 1, STEPS - step)
        for ref, coef_at, triples in work:
            coefs = load_coefs(ref, coef_at + row)
            for triple in triples:
                new = step_tile(src[triple], read_at, WEDGE, coefs)
                for v in range(3):
                    dst[triple][pl.ds(wedge_at + v * WEDGE, TILE), :] = new[v]
        if step < STEPS:
            lean(step)

    done = refs[STEPS % 2]
    place = in_strip()
    lanes = lane_ids()
    edge = (lanes < HALO) | (lanes >= LANES - HALO)
    full = members // SLOTS
    for v in range(3):

        def strip(g):
            return done[members + g][pl.ds(wedge_at + v * WEDGE, TILE), :]

        for q in range(full + 1):
            west, east = (strip(q), strip(full + q)) if q < full else (strip(2 * full), rotate(strip(2 * full), -MIX))
            both = jnp.where((place >= HALO) & (place < 2 * HALO), west, east)
            for s in range(min(SLOTS, members - SLOTS * q)):
                m = SLOTS * q + s
                inner = done[m][pl.ds(wedge_at + v * WEDGE, TILE), :]
                fields[m, v] = jnp.where(edge, rotate(both, -STRIP * s - HALO), inner)
    for i in range(members):
        for j in range(i, members):
            at = TILE * pair_place(i, j, members)
            pairs[at : at + TILE, :] = (
                fields[i, 0] * fields[j, 0] + fields[i, 1] * fields[j, 1] + fields[i, 2] * fields[j, 2]
            )
    half = members // 2
    sums = []
    for a in range(members + 1):
        for b in range(half, TILE):
            at = TILE * (TILE * a + b)
            pairs[at : at + TILE, :] = jnp.zeros((TILE, LANES), f32)
        total = pairs[pl.ds(TILE * TILE * a, TILE, stride=TILE), :]
        for s in range(1, TILE):
            total = total + pairs[pl.ds(TILE * TILE * a + s, TILE, stride=TILE), :]
        sums.append(total)
    if is_a:
        for a in range(members + 1):
            result[TILE * a : TILE * a + TILE, :] = sums[a]
    else:
        packed = jnp.zeros((TILE, LANES), f32)
        for a in range(members + 1):
            total = jnp.sum(sums[a] + partial_in[TILE * a : TILE * a + TILE, :], axis=1, keepdims=True)
            packed = jnp.where(lanes == a, total, packed)
        packed = pltpu.roll(packed, 0, axis=1, stride=SPREAD, stride_axis=0)
        result[...] = jnp.broadcast_to(jnp.sum(packed, axis=0, keepdims=True), result.shape)


SPREAD = LANES // TILE


def pair_place(i, j, members):
    b = min(i, members - 1 - i)
    a = j - b if i == b else j + 1
    return TILE * a + b


def first_side_kernel(members, own, halo, facts, hist_c, hist_e, strip_base, fields, result, *scratch):
    side_kernel(members, True, own, halo, facts, hist_c, hist_e, strip_base, None, fields, result, *scratch)


def finish_kernel(members, count, fields_a, fields_b, got, out, factor_out, done, factor, sems):
    total = got[0:TILE, :]
    for r in range(TILE, got.shape[0], TILE):
        total = total + got[r : r + TILE, :]
    packed = jnp.sum(total, axis=0, keepdims=True) / count
    packed = jnp.broadcast_to(packed, (TILE, LANES))
    gram = {}
    for i in range(members):
        for j in range(i, members):
            place = pair_place(i, j, members)
            lane = SPREAD * (place % TILE) + place // TILE
            gram[i, j] = jnp.broadcast_to(packed[:, lane : lane + 1], (TILE, LANES))
    a_at = pl.multiple_of(jnp.where(is_even("lat"), TILE, 0), TILE)
    places = [a_at, pl.multiple_of(TILE - a_at, TILE)]
    x = [[[ref[m, v] for v in range(3)] for ref in (fields_a, fields_b)] for m in range(members)]
    lanes = lane_ids()
    copies = []
    for k in range(members):
        scale = lax.rsqrt(gram[k, k])
        for half in range(2):
            for v in range(3):
                x[k][half][v] = x[k][half][v] * scale
                done[k, v, pl.ds(places[half], TILE), :] = x[k][half][v]
        copy = pltpu.make_async_copy(done.at[k], out.at[k], sems.at[k])
        copy.start()
        copies.append(copy)
        row = jnp.zeros((TILE, LANES), f32)
        for i in range(k, members):
            gram[k, i] = gram[k, i] * scale
            row = jnp.where(lanes == i, gram[k, i], row)
        factor[k : k + 1, :] = row[0:1, :members]
        for i in range(k + 1, members):
            for j in range(i, members):
                gram[i, j] = gram[i, j] - gram[k, i] * gram[k, j]
            for half in range(2):
                for v in range(3):
                    x[i][half][v] = x[i][half][v] - gram[k, i] * x[k][half][v]
    copy = pltpu.make_async_copy(factor, factor_out, sems.at[members])
    copy.start()
    for copy in copies + [copy]:
        copy.wait()


def swap(block, axis, count, even_up, periodic):
    pairs = []
    for i in range(count):
        other = i + 1 if (i % 2 == 0) == even_up else i - 1
        if periodic:
            other %= count
        if 0 <= other < count:
            pairs.append((i, other))
    return lax.ppermute(block, axis, pairs)


def shape(*dims):
    return jax.ShapeDtypeStruct(dims, f32)


def cost(flops):
    return pl.CostEstimate(flops=flops, bytes_accessed=1_000_000, transcendentals=0)


def per_device(perturbations, base_wind, base_height):
    members, _, rows, cols = perturbations.shape
    n_lat, n_lon = lax.axis_size("lat"), lax.axis_size("lon")
    total_rows, total_cols = rows * n_lat, cols * n_lon
    groups = len(strip_kinds(members))
    planes_c, planes_e = 3 * members, 3 * groups

    own, msg_a, msg_b = pl.pallas_call(
        functools.partial(load_kernel, members),
        out_shape=[shape(members + 1, 3, rows, LANES), shape(3, rows, LANES), shape(3, rows, LANES)],
        in_specs=[HBM] * 3,
        out_specs=[VMEM] * 3,
        scratch_shapes=[pltpu.SemaphoreType.DMA((6,))],
        compiler_params=PARAMS,
        name="load",
    )(*(pltpu.with_memory_space_constraint(x, pltpu.HBM) for x in (perturbations, base_wind, base_height)))
    got_b = swap(msg_b, "lon", n_lon, False, True)
    got_a = swap(msg_a, "lon", n_lon, True, True)

    facts, hist_c = pl.pallas_call(
        functools.partial(centre_kernel, members, total_rows),
        out_shape=[shape(2, FACTS, LANES), shape(2, STEPS, planes_c, TILE, LANES)],
        in_specs=[VMEM],
        out_specs=[VMEM] * 2,
        scratch_shapes=[
            pltpu.VMEM((FRONT + planes_c * PYRAMID, LANES), f32),
            pltpu.VMEM((FRONT + planes_c * PYRAMID, LANES), f32),
            pltpu.VMEM((FRONT + 3 * PYRAMID, LANES), f32),
            pltpu.VMEM((NCOEF * FACTS, LANES), f32),
        ],
        compiler_params=PARAMS,
        cost_estimate=cost(3_000_000),
        name="centre",
    )(own)

    send = shape(3 * members + 9, TILE, LANES)
    send_a, send_b, west, east = pl.pallas_call(
        functools.partial(meet_kernel, members),
        out_shape=[send, send, shape(3, rows, LANES), shape(3, rows, LANES)],
        in_specs=[VMEM] * 4,
        out_specs=[VMEM] * 4,
        compiler_params=PARAMS,
        name="meet",
    )(own, got_b, got_a, facts)
    halo_a = swap(send_a, "lat", n_lat, True, False)
    halo_b = swap(send_b, "lat", n_lat, False, False)

    hist_e, strip_base = pl.pallas_call(
        functools.partial(edges_kernel, members),
        out_shape=[shape(2, STEPS, planes_e, TILE, LANES), shape(KINDS, 3, rows, LANES)],
        in_specs=[VMEM] * 4,
        out_specs=[VMEM] * 2,
        scratch_shapes=[
            pltpu.VMEM((FRONT + planes_e * PYRAMID, LANES), f32),
            pltpu.VMEM((FRONT + planes_e * PYRAMID, LANES), f32),
            pltpu.VMEM((FRONT + 3 * KINDS * PYRAMID, LANES), f32),
            pltpu.VMEM((KINDS * NCOEF * FACTS, LANES), f32),
        ],
        compiler_params=PARAMS,
        cost_estimate=cost(2_000_000),
        name="edges",
    )(own, west, east, facts)

    wedges = [
        pltpu.VMEM((3 * BASE, LANES), f32),
        pltpu.VMEM((3 * KINDS * BASE, LANES), f32),
        pltpu.VMEM((NCOEF * FACTS, LANES), f32),
        pltpu.VMEM((KINDS * NCOEF * FACTS, LANES), f32),
        pltpu.VMEM((TILE * LANES, LANES), f32),
    ] + [pltpu.VMEM((3 * WEDGE, LANES), f32)] * (2 * (members + groups))
    half = shape(members, 3, TILE, LANES)
    fields_a, partial = pl.pallas_call(
        functools.partial(first_side_kernel, members),
        out_shape=[half, shape((members + 1) * TILE, LANES)],
        in_specs=[VMEM] * 6,
        out_specs=[VMEM] * 2,
        scratch_shapes=wedges,
        compiler_params=PARAMS,
        cost_estimate=cost(4_000_000),
        name="side_a",
    )(own, halo_a, facts, hist_c, hist_e, strip_base)
    fields_b, send_gram = pl.pallas_call(
        functools.partial(side_kernel, members, False),
        out_shape=[half, shape(n_lat * n_lon, LANES)],
        in_specs=[VMEM] * 7,
        out_specs=[VMEM] * 2,
        scratch_shapes=wedges,
        compiler_params=PARAMS,
        cost_estimate=cost(4_000_000),
        name="side_b",
    )(own, halo_b, facts, hist_c, hist_e, strip_base, partial)

    got = lax.all_to_all(send_gram, ("lon", "lat"), 0, 0, tiled=True)

    return pl.pallas_call(
        functools.partial(finish_kernel, members, float(3 * total_rows * total_cols)),
        out_shape=[shape(*perturbations.shape), shape(members, members)],
        in_specs=[VMEM] * 3,
        out_specs=[HBM, HBM],
        scratch_shapes=[
            pltpu.VMEM(perturbations.shape, f32),
            pltpu.VMEM((members, members), f32),
            pltpu.SemaphoreType.DMA((members + 1,)),
        ],
        compiler_params=PARAMS,
        name="finish",
    )(fields_a, fields_b, got)


def solution(mesh):
    return jax.shard_map(
        per_device,
        mesh=mesh,
        in_specs=(P(None, None, "lat", "lon"), P(None, "lat", "lon"), P("lat", "lon")),
        out_specs=(P(None, None, "lat", "lon"), P()),
        check_vma=False,
    )
```

```python
import functools
import math

import jax
import jax.numpy as jnp
from jax import lax
from jax.experimental import pallas as pl
from jax.experimental.pallas import tpu as pltpu
from jax.sharding import PartitionSpec as P

STEPS = 8
HALO = STEPS
TILE = 8
LANES = 128
FACTS = 40
STRIP = 3 * HALO
SLOTS = LANES // STRIP
MIX = 2 * STRIP + HALO
KINDS = 3
NCOEF = 18
SPARE = 3

advect_rate = 0.1
turn_rate = 0.5
gravity_rate = 0.2
diffuse_rate = 0.12

f32 = jnp.float32
VMEM = pl.BlockSpec(memory_space=pltpu.VMEM)
HBM = pl.BlockSpec(memory_space=pltpu.HBM)
PARAMS = pltpu.CompilerParams(vmem_limit_bytes=40 * 1024 * 1024)


def rotate(x, amount):
    amount = amount % LANES
    return x if amount == 0 else pltpu.roll(x, amount, axis=x.ndim - 1)


def lane_ids(rows=TILE):
    return lax.broadcasted_iota(jnp.int32, (rows, LANES), 1)


def dynamic_zero():
    return jnp.minimum(lax.axis_index("lat"), 0)


def is_inner():
    lat = lax.axis_index("lat")
    return jnp.where((lat > 0) & (lat < lax.axis_size("lat") - 1), 1, 0)


def is_north(last):
    toward_a = 1 - is_inner() if last else is_inner()
    return lax.rem(toward_a + lax.axis_index("lat"), 2) == 0


def is_even(axis):
    return lax.rem(lax.axis_index(axis), 2) == 0


def store_coefs(base, at, stride, facts, facts_at, coef, coef_at, tiles):
    half = 0.5 * advect_rate
    for t in tiles:
        m = facts[0, pl.ds(facts_at + TILE * t, TILE), :]
        turn = facts[1, pl.ds(facts_at + TILE * t, TILE), :]

        def three(v):
            return [base[pl.ds(at + v * stride + TILE * t + d, TILE), :] for d in range(3)]

        us, u, un = three(0)
        vs, v, vn = three(1)
        hs, h, hn = three(2)
        ue, ve, he = rotate(u, -1), rotate(v, -1), rotate(h, -1)
        uw, vw, hw = rotate(u, 1), rotate(v, 1), rotate(h, 1)
        centre = (1.0 - 4.0 * diffuse_rate) * m
        dif = diffuse_rate * m
        am = half * m
        values = [
            dif - am * u,
            dif + am * u,
            dif - am * v,
            dif + am * v,
            centre - am * (ue - uw),
            turn - am * (un - us),
            centre - am * (vn - vs),
            -turn - am * (ve - vw),
            (0.5 * gravity_rate) * m,
            dif - am * ue,
            dif + am * uw,
            dif - am * vn,
            dif + am * vs,
            -am * he,
            am * hw,
            -am * hn,
            am * hs,
            centre,
        ]
        for i, value in enumerate(values):
            coef[pl.ds(coef_at + i * FACTS + TILE * t, TILE), :] = value


def load_coefs(coef, at):
    return [coef[pl.ds(at + i * FACTS, TILE), :] for i in range(NCOEF)]


def step_tile(src, at, stride, coefs):
    (ae, aw, an, as_, cu, du, cv, dv, k1, he, hw, hn, hs, ue, uw, vn, vs, c0) = coefs

    def three(v):
        return [src[pl.ds(at + v * stride + d, TILE), :] for d in range(3)]

    u_s, u, u_n = three(0)
    v_s, v, v_n = three(1)
    h_s, h, h_n = three(2)
    u_e, v_e, h_e = rotate(u, -1), rotate(v, -1), rotate(h, -1)
    u_w, v_w, h_w = rotate(u, 1), rotate(v, 1), rotate(h, 1)
    new_u = (ae * u_e + aw * u_w) + (an * u_n + as_ * u_s) + (cu * u + du * v) + k1 * (h_w - h_e)
    new_v = (ae * v_e + aw * v_w) + (an * v_n + as_ * v_s) + (cv * v + dv * u) + k1 * (h_s - h_n)
    new_h = (he * h_e + hw * h_w) + (hn * h_n + hs * h_s) + (ue * u_e + uw * u_w) + (vn * v_n + vs * v_s) + c0 * h
    return new_u, new_v, new_h


PYRAMID = 24
FRONT = 8


def pyramid(refs, zero, work, hist):
    def keep(step, source, plane):
        start = zero + FRONT + plane * PYRAMID
        hist[0, step, plane] = source[pl.ds(start, TILE), :]
        hist[1, step, plane] = source[pl.ds(start + TILE - 2 * step, TILE), :]

    for step in range(1, STEPS):
        src, dst = refs[(step - 1) % 2], refs[step % 2]
        for t in range(-(-(16 - 2 * step) // TILE)):
            for coef, coef_at, triples in work:
                coefs = load_coefs(coef, coef_at + TILE * t + step - 1)
                for triple in triples:
                    at = FRONT + 3 * triple * PYRAMID + TILE * t
                    new = step_tile(src, zero + at, PYRAMID, coefs)
                    for v in range(3):
                        dst[pl.ds(zero + at + v * PYRAMID, TILE), :] = new[v]
        for _, _, triples in work:
            for triple in triples:
                for v in range(3):
                    keep(step, dst, 3 * triple + v)


def first_level(hist, plane, low, high):
    hist[0, 0, plane] = low
    hist[1, 0, plane] = high


def slot_range(s, shift):
    lanes = (lane_ids() + shift) % LANES
    return (lanes >= STRIP * s) & (lanes < STRIP * s + STRIP)


def in_strip():
    return lane_ids() % STRIP


def own_strips(rows_of, members):
    wests, easts = [], []
    for q in range(members // SLOTS):
        west = east = None
        for s in range(SLOTS):
            moved = rotate(rows_of(SLOTS * q + s), STRIP * s + HALO)
            west = moved if s == 0 else jnp.where(slot_range(s, 0), moved, west)
            east = moved if s == 0 else jnp.where(slot_range(s, HALO), moved, east)
        wests.append(west)
        easts.append(east)
    left = members % SLOTS
    mixed = None
    for s in range(2 * left):
        moved = rotate(rows_of(members - left + s % left), STRIP * s + (HALO if s < left else 2 * HALO))
        mixed = moved if s == 0 else jnp.where(slot_range(s, 0), moved, mixed)
    return wests + easts + [mixed]


def fill_strips(vectors, west_halo, east_halo, members):
    place = in_strip()
    full, left = members // SLOTS, members % SLOTS
    filled = []
    for q in range(full):
        filled.append(jnp.where(place < HALO, rotate(west_halo, -HALO * q), vectors[q]))
    inner = (place >= HALO) & (place < 2 * HALO)
    for q in range(full):
        filled.append(jnp.where(inner, rotate(east_halo, -HALO * q), vectors[full + q]))
    lanes = lane_ids()
    mixed = jnp.where((place < HALO) & (lanes < left * STRIP), rotate(west_halo, -HALO * full), vectors[-1])
    outer = (place >= 2 * HALO) & (lanes >= left * STRIP)
    return filled + [jnp.where(outer, rotate(east_halo, MIX - HALO * full), mixed)]


def base_strips(rows, west_halo, east_halo, members):
    q, left = members // SLOTS, members % SLOTS
    place = in_strip()
    lanes = lane_ids()
    west = east = mixed = None
    for s in range(SLOTS):
        moved = rotate(rows, STRIP * s + HALO)
        west = moved if s == 0 else jnp.where(slot_range(s, 0), moved, west)
        east = moved if s == 0 else jnp.where(slot_range(s, HALO), moved, east)
        if s < 2 * left:
            over = moved if s < left else rotate(rows, STRIP * s + 2 * HALO)
            mixed = over if s == 0 else jnp.where(slot_range(s, 0), over, mixed)
    near = [rotate(halo, -HALO * q) for halo in (west_halo, east_halo)]
    far = [rotate(halo, -HALO * q - STRIP * left) for halo in (west_halo, east_halo)]
    low = lanes < left * STRIP
    west = jnp.where(place < HALO, jnp.where(low, far[0], near[0]), west)
    inner = (place >= HALO) & (place < 2 * HALO)
    east = jnp.where(inner, jnp.where(lanes < left * STRIP + HALO, far[1], near[1]), east)
    mixed = jnp.where((place < HALO) & low, far[0], mixed)
    outer = (place >= 2 * HALO) & (lanes >= left * STRIP)
    return west, east, jnp.where(outer, rotate(east_halo, MIX - HALO * q - STRIP * left), mixed)


def strip_kinds(members):
    full = members // SLOTS
    return [0] * full + [1] * full + [2]


def load_kernel(members, pert, wind, height, own, main_a, msg_a, msg_b, sems):
    chunk = members // 4
    copies = [
        pltpu.make_async_copy(wind, own.at[members, pl.ds(0, 2)], sems.at[0]),
        pltpu.make_async_copy(height, own.at[members, 2], sems.at[1]),
    ]
    for i in range(4):
        part = pl.ds(i * chunk, chunk)
        copies.append(pltpu.make_async_copy(pert.at[part], own.at[part], sems.at[2 + i]))
    for copy in copies:
        copy.start()
    for copy in copies:
        copy.wait()
    low = pl.multiple_of(jnp.where(is_even("lat"), TILE, 0), TILE)
    for m in range(SPARE):
        main_a[members + 1 + m] = jnp.zeros((3, TILE, LANES), f32)
    for m in range(members + 1):
        for v in range(3):
            main_a[m, v] = own[m, v, pl.ds(low, TILE), :]
    lon_even = is_even("lon")
    lanes = lane_ids()
    for v in range(3):
        for t in range(2):
            rows = slice(TILE * t, TILE * t + TILE)
            to_e = to_w = None
            for q in range(3):
                for s in range(SLOTS):
                    low = STRIP * s + HALO * q
                    moved = rotate(own[min(SLOTS * q + s, members), v, rows, :], low + HALO)
                    if to_e is None:
                        to_e = to_w = moved
                    else:
                        to_e = jnp.where((lanes >= low) & (lanes < low + HALO), moved, to_e)
                        to_w = jnp.where((lanes >= low + HALO) & (lanes < low + 2 * HALO), moved, to_w)
            msg_a[v, rows, :] = jnp.where(lon_even, to_e, to_w)
            msg_b[v, rows, :] = jnp.where(lon_even, to_w, to_e)


def centre_kernel(members, total_rows, own, facts, hist, first, second, base, coef):
    zero = dynamic_zero()
    start = lax.axis_index("lat") * 16 - HALO + 1
    for t in range(FACTS // TILE):
        glob = start + TILE * t + lax.broadcasted_iota(jnp.int32, (TILE, LANES), 0)
        inside = ((glob >= 0) & (glob < total_rows)).astype(f32)
        rows = slice(TILE * t, TILE * t + TILE)
        facts[0, rows, :] = inside
        facts[1, rows, :] = turn_rate * inside * jnp.sin(math.pi * ((glob.astype(f32) + 0.5) / total_rows - 0.5))
    for m in range(members + 1):
        for v in range(3):
            low, high = own[m, v, 0:TILE, :], own[m, v, TILE:16, :]
            plane = 3 * m + v
            if m < members:
                ref, at = first, FRONT + plane * PYRAMID
                first_level(hist, plane, low, high)
            else:
                ref, at = base, FRONT + v * PYRAMID
            ref[at : at + TILE, :] = low
            ref[at + TILE : at + 16, :] = high
    store_coefs(base, zero + FRONT, PYRAMID, facts, HALO, coef, zero, range(2))
    pyramid([first, second], zero, [(coef, zero, list(range(members)))], hist)


def meet_kernel(members, own, got_b, got_a, send_b, west, east, corners):
    lon_even = is_even("lon")
    low = pl.multiple_of(jnp.where(is_even("lat"), 0, TILE), TILE)
    for v in range(3):
        for t in range(2):
            rows = slice(TILE * t, TILE * t + TILE)
            west[v, rows, :] = jnp.where(lon_even, got_b[v, rows, :], got_a[v, rows, :])
            east[v, rows, :] = jnp.where(lon_even, got_a[v, rows, :], got_b[v, rows, :])
    for m in range(members + 1):
        for v in range(3):
            send_b[m, v] = own[m, v, pl.ds(low, TILE), :]
    for v in range(3):
        for side, halo in enumerate((west, east)):
            send_b[members + 1 + side, v] = halo[v, pl.ds(low, TILE), :]
            corners[side, v] = halo[v, pl.ds(pl.multiple_of(TILE - low, TILE), TILE), :]


def edges_kernel(members, own, west, east, facts, hist, strip_base, first, second, base, coef):
    zero = dynamic_zero()
    kinds = strip_kinds(members)
    for v in range(3):
        for t in range(2):
            rows = slice(TILE * t, TILE * t + TILE)
            halos = west[v, rows, :], east[v, rows, :]
            strips = fill_strips(own_strips(lambda m: own[m, v, rows, :], members), *halos, members)
            for g, strip in enumerate(strips):
                at = FRONT + (3 * g + v) * PYRAMID + TILE * t
                first[at : at + TILE, :] = strip
                hist[t, 0, 3 * g + v] = strip
            for kind, strip in enumerate(base_strips(own[members, v, rows, :], *halos, members)):
                at = FRONT + (3 * kind + v) * PYRAMID + TILE * t
                base[at : at + TILE, :] = strip
                strip_base[kind, v, rows, :] = strip
    work = []
    for kind in range(KINDS):
        coef_at = zero + kind * NCOEF * FACTS
        store_coefs(base, zero + FRONT + 3 * kind * PYRAMID, PYRAMID, facts, HALO, coef, coef_at, range(2))
        work.append((coef, coef_at, [g for g in range(len(kinds)) if kinds[g] == kind]))
    pyramid([first, second], zero, work, hist)


WEDGE = 16
BASE = 40


class Side:
    def __init__(self, last):
        north = is_north(last)
        self.north = north
        self.index = jnp.where(north, 0, 1)
        self.wedge_at = jnp.where(north, 0, TILE)
        self.lean_at = jnp.where(north, TILE, 0)
        self.read_at = jnp.where(north, 0, TILE - 2)
        self.own_at = jnp.where(north, 2 * TILE, 1)
        self.halo_at = jnp.where(north, TILE, 2 * TILE + 1)
        self.facts_at = jnp.where(north, 0, 2 * TILE - 1)
        self.zero = dynamic_zero()

    def wedge(self, v):
        return pl.ds(self.wedge_at + v * WEDGE, TILE)

    def put_base(self, base, plane, own, halo):
        for t in range(2):
            base[pl.ds(self.own_at + plane * BASE + TILE * t, TILE), :] = own(t)
        base[pl.ds(self.halo_at + plane * BASE, TILE), :] = halo

    def coefs(self, base, kind, facts, coef):
        coef_at = self.zero + kind * NCOEF * FACTS
        at = self.zero + TILE + 3 * kind * BASE
        store_coefs(base, at, BASE, facts, self.facts_at, coef, coef_at, range(2))
        return coef_at


def prepare_centre(side, members, own, halo, facts, base, coef, first):
    for m in range(members):
        for v in range(3):
            first[m][side.wedge(v), :] = halo(m, v)
    for v in range(3):
        side.put_base(base, v, lambda t: own[members, v, TILE * t : TILE * t + TILE, :], halo(members, v))
    return [(coef, side.coefs(base, 0, facts, coef), list(range(members)))]


def prepare_edges(side, members, halo, corner, facts, strip_base, base, coef, first):
    kinds = strip_kinds(members)
    for v in range(3):
        west, east = corner(v)
        strips = fill_strips(own_strips(lambda m: halo(m, v), members), west, east, members)
        for g, strip in enumerate(strips):
            first[members + g][side.wedge(v), :] = strip
        for kind, strip in enumerate(base_strips(halo(members, v), west, east, members)):
            side.put_base(base, 3 * kind + v, lambda t: strip_base[kind, v, TILE * t : TILE * t + TILE, :], strip)
    return [
        (coef, side.coefs(base, kind, facts, coef), [members + g for g in range(len(kinds)) if kinds[g] == kind])
        for kind in range(KINDS)
    ]


def run_wedges(members, jobs):
    def lean(job, step):
        side, work, hist_c, hist_e, *refs = job
        for _, _, part in work:
            for triple in part:
                hist, plane = (hist_c, 3 * triple) if triple < members else (hist_e, 3 * (triple - members))
                for v in range(3):
                    refs[step % 2][triple][pl.ds(side.lean_at + v * WEDGE, TILE), :] = hist[side.index, step, plane + v]

    for job in jobs:
        lean(job, 0)
    for step in range(1, STEPS + 1):
        for job in jobs:
            side, work, _, _, *refs = job
            src, dst = refs[(step - 1) % 2], refs[step % 2]
            row = jnp.where(side.north, step - 1, STEPS - step)
            for ref, coef_at, part in work:
                coefs = load_coefs(ref, coef_at + row)
                for triple in part:
                    new = step_tile(src[triple], side.read_at, WEDGE, coefs)
                    for v in range(3):
                        dst[triple][side.wedge(v), :] = new[v]
            if step < STEPS:
                lean(job, step)


def merge(side, members, done, inner, fields):
    place = in_strip()
    lanes = lane_ids()
    edge = (lanes < HALO) | (lanes >= LANES - HALO)
    full = members // SLOTS
    for v in range(3):

        def strip(g):
            return done[members + g][side.wedge(v), :]

        for q in range(full + 1):
            west, east = (strip(q), strip(full + q)) if q < full else (strip(2 * full), rotate(strip(2 * full), -MIX))
            both = jnp.where((place >= HALO) & (place < 2 * HALO), west, east)
            for s in range(min(SLOTS, members - SLOTS * q)):
                m = SLOTS * q + s
                fields[m, v] = jnp.where(edge, rotate(both, -STRIP * s - HALO), inner(m, v))


def pair_sums(members, fields_1, fields_2, pairs):
    for i in range(members):
        for j in range(i, members):
            at = TILE * pair_place(i, j, members)
            products = [ref[i, v] * ref[j, v] for ref in (fields_1, fields_2) for v in range(3)]
            pairs[at : at + TILE, :] = sum(products[1:], products[0])
    sums = []
    for a in range(members + 1):
        for b in range(members // 2, TILE):
            at = TILE * (TILE * a + b)
            pairs[at : at + TILE, :] = jnp.zeros((TILE, LANES), f32)
        total = pairs[pl.ds(TILE * TILE * a, TILE, stride=TILE), :]
        for s in range(1, TILE):
            total = total + pairs[pl.ds(TILE * TILE * a + s, TILE, stride=TILE), :]
        sums.append(total)
    return sums


def centre_side(side, members, own, halo, facts, hist_c, centre, base, coef, wedges):
    first, second = wedges[:members], wedges[members:]
    work = prepare_centre(side, members, own, halo, facts, base, coef, first)
    run_wedges(members, [(side, work, hist_c, None, first, second)])
    for m in range(members):
        for v in range(3):
            centre[m, v] = first[m][side.wedge(v), :]


def first_rows(halo_a):
    inner = is_inner() == 1
    return lambda m, v: jnp.where(inner, halo_a[m, v], 0.0)


def last_rows(halo_a, halo_b):
    inner = is_inner() == 1
    return lambda m, v: jnp.where(inner, halo_b[m, v], halo_a[m, v])


def first_centre_kernel(members, own, halo_a, facts, hist_c, centre, base, coef, *wedges):
    centre_side(Side(False), members, own, first_rows(halo_a), facts, hist_c, centre, base, coef, wedges)


def last_centre_kernel(members, own, halo_a, halo_b, facts, hist_c, centre, base, coef, *wedges):
    centre_side(Side(True), members, own, last_rows(halo_a, halo_b), facts, hist_c, centre, base, coef, wedges)


def edges_of_sides_kernel(
    members, centre_1, centre_2, halo_a, halo_b, corners, facts, hist_e, strip_base, fields_1, fields_2, result, *scratch
):
    inner = is_inner() == 1
    bases, coefs, pairs, wedges = scratch[0:2], scratch[2:4], scratch[4], scratch[5:]
    groups = len(wedges) // 4

    def corner_first(v):
        return tuple(jnp.where(inner, corners[i, v], 0.0) for i in range(2))

    def corner_last(v):
        return tuple(jnp.where(inner, halo_b[members + 1 + i, v], corners[i, v]) for i in range(2))

    jobs = []
    halos = (first_rows(halo_a), corner_first), (last_rows(halo_a, halo_b), corner_last)
    for n, (halo, corner) in enumerate(halos):
        side = Side(n == 1)
        part = wedges[2 * n * groups : 2 * (n + 1) * groups]
        first = {members + g: part[g] for g in range(groups)}
        second = {members + g: part[groups + g] for g in range(groups)}
        work = prepare_edges(side, members, halo, corner, facts, strip_base, bases[n], coefs[n], first)
        jobs.append((side, work, None, hist_e, first, second))
    run_wedges(members, jobs)
    for n, (centre, fields) in enumerate(((centre_1, fields_1), (centre_2, fields_2))):
        merge(jobs[n][0], members, jobs[n][4], lambda m, v: centre[m, v], fields)
    sums = pair_sums(members, fields_1, fields_2, pairs)
    lanes = lane_ids()
    packed = jnp.zeros((TILE, LANES), f32)
    for a, total in enumerate(sums):
        packed = jnp.where(lanes == a, jnp.sum(total, axis=1, keepdims=True), packed)
    packed = pltpu.roll(packed, 0, axis=1, stride=SPREAD, stride_axis=0)
    result[...] = jnp.broadcast_to(jnp.sum(packed, axis=0, keepdims=True), result.shape)


SPREAD = LANES // TILE


def pair_place(i, j, members):
    b = min(i, members - 1 - i)
    a = j - b if i == b else j + 1
    return TILE * a + b


def finish_kernel(members, count, fields_a, fields_b, got, out, factor_out, done, factor, sems):
    total = got[0:TILE, :]
    for r in range(TILE, got.shape[0], TILE):
        total = total + got[r : r + TILE, :]
    packed = jnp.sum(total, axis=0, keepdims=True) / count
    packed = jnp.broadcast_to(packed, (TILE, LANES))
    gram = {}
    for i in range(members):
        for j in range(i, members):
            place = pair_place(i, j, members)
            lane = SPREAD * (place % TILE) + place // TILE
            gram[i, j] = jnp.broadcast_to(packed[:, lane : lane + 1], (TILE, LANES))
    first_at = pl.multiple_of(jnp.where(is_north(False), 0, TILE), TILE)
    places = [first_at, pl.multiple_of(TILE - first_at, TILE)]
    x = [[[ref[m, v] for v in range(3)] for ref in (fields_a, fields_b)] for m in range(members)]
    lanes = lane_ids()
    copies = []
    for k in range(members):
        scale = lax.rsqrt(gram[k, k])
        for half in range(2):
            for v in range(3):
                x[k][half][v] = x[k][half][v] * scale
                done[k, v, pl.ds(places[half], TILE), :] = x[k][half][v]
        copy = pltpu.make_async_copy(done.at[k], out.at[k], sems.at[k])
        copy.start()
        copies.append(copy)
        row = jnp.zeros((TILE, LANES), f32)
        for i in range(k, members):
            gram[k, i] = gram[k, i] * scale
            row = jnp.where(lanes == i, gram[k, i], row)
        factor[k : k + 1, :] = row[0:1, :members]
        for i in range(k + 1, members):
            for j in range(i, members):
                gram[i, j] = gram[i, j] - gram[k, i] * gram[k, j]
            for half in range(2):
                for v in range(3):
                    x[i][half][v] = x[i][half][v] - gram[k, i] * x[k][half][v]
    copy = pltpu.make_async_copy(factor, factor_out, sems.at[members])
    copy.start()
    for copy in copies + [copy]:
        copy.wait()


def swap(block, axis, count, even_up, periodic):
    pairs = []
    for i in range(count):
        other = i + 1 if (i % 2 == 0) == even_up else i - 1
        if periodic:
            other %= count
        if 0 <= other < count:
            pairs.append((i, other))
    return lax.ppermute(block, axis, pairs)


def shape(*dims):
    return jax.ShapeDtypeStruct(dims, f32)


def cost(micros):
    return pl.CostEstimate(flops=0, bytes_accessed=int(micros * 3.6e6), transcendentals=0)


def per_device(perturbations, base_wind, base_height):
    members, _, rows, cols = perturbations.shape
    n_lat, n_lon = lax.axis_size("lat"), lax.axis_size("lon")
    total_rows, total_cols = rows * n_lat, cols * n_lon
    groups = len(strip_kinds(members))
    planes_c, planes_e = 3 * members, 3 * groups

    own, main_a, msg_a, msg_b = pl.pallas_call(
        functools.partial(load_kernel, members),
        out_shape=[
            shape(members + 1, 3, rows, LANES),
            shape(members + 1 + SPARE, 3, TILE, LANES),
            shape(3, rows, LANES),
            shape(3, rows, LANES),
        ],
        in_specs=[HBM] * 3,
        out_specs=[VMEM] * 4,
        scratch_shapes=[pltpu.SemaphoreType.DMA((6,))],
        compiler_params=PARAMS,
        name="load",
    )(*(pltpu.with_memory_space_constraint(x, pltpu.HBM) for x in (perturbations, base_wind, base_height)))
    halo_a = swap(main_a, "lat", n_lat, True, False)
    got_b = swap(msg_b, "lon", n_lon, False, True)
    got_a = swap(msg_a, "lon", n_lon, True, True)

    facts, hist_c = pl.pallas_call(
        functools.partial(centre_kernel, members, total_rows),
        out_shape=[shape(2, FACTS, LANES), shape(2, STEPS, planes_c, TILE, LANES)],
        in_specs=[VMEM],
        out_specs=[VMEM] * 2,
        scratch_shapes=[
            pltpu.VMEM((FRONT + planes_c * PYRAMID, LANES), f32),
            pltpu.VMEM((FRONT + planes_c * PYRAMID, LANES), f32),
            pltpu.VMEM((FRONT + 3 * PYRAMID, LANES), f32),
            pltpu.VMEM((NCOEF * FACTS, LANES), f32),
        ],
        compiler_params=PARAMS,
        cost_estimate=cost(20),
        name="centre",
    )(own)

    send_b, west, east, corners = pl.pallas_call(
        functools.partial(meet_kernel, members),
        out_shape=[
            shape(members + 3, 3, TILE, LANES),
            shape(3, rows, LANES),
            shape(3, rows, LANES),
            shape(2, 3, TILE, LANES),
        ],
        in_specs=[VMEM] * 3,
        out_specs=[VMEM] * 4,
        compiler_params=PARAMS,
        cost_estimate=cost(0.01),
        name="meet",
    )(own, got_b, got_a)
    halo_b = swap(send_b, "lat", n_lat, False, False)
    corners = swap(corners, "lat", n_lat, True, False)

    hist_e, strip_base = pl.pallas_call(
        functools.partial(edges_kernel, members),
        out_shape=[shape(2, STEPS, planes_e, TILE, LANES), shape(KINDS, 3, rows, LANES)],
        in_specs=[VMEM] * 4,
        out_specs=[VMEM] * 2,
        scratch_shapes=[
            pltpu.VMEM((FRONT + planes_e * PYRAMID, LANES), f32),
            pltpu.VMEM((FRONT + planes_e * PYRAMID, LANES), f32),
            pltpu.VMEM((FRONT + 3 * KINDS * PYRAMID, LANES), f32),
            pltpu.VMEM((KINDS * NCOEF * FACTS, LANES), f32),
        ],
        compiler_params=PARAMS,
        cost_estimate=cost(0.01),
        name="edges",
    )(own, west, east, facts)

    def scratch(bases, triples, with_pairs):
        shapes = [(3 * n * BASE, LANES) for n in bases] + [(n * NCOEF * FACTS, LANES) for n in bases]
        shapes += [(TILE * LANES, LANES)] * with_pairs + [(3 * WEDGE, LANES)] * (2 * triples)
        return [pltpu.VMEM(dims, f32) for dims in shapes]

    half = shape(members, 3, TILE, LANES)
    centre_first = pl.pallas_call(
        functools.partial(first_centre_kernel, members),
        out_shape=half,
        in_specs=[VMEM] * 4,
        out_specs=VMEM,
        scratch_shapes=scratch([1], members, 0),
        compiler_params=PARAMS,
        cost_estimate=cost(0.01),
        name="first_centre",
    )(own, halo_a, facts, hist_c)
    centre_last = pl.pallas_call(
        functools.partial(last_centre_kernel, members),
        out_shape=half,
        in_specs=[VMEM] * 5,
        out_specs=VMEM,
        scratch_shapes=scratch([1], members, 0),
        compiler_params=PARAMS,
        cost_estimate=cost(0.01),
        name="last_centre",
    )(own, halo_a, halo_b, facts, hist_c)
    fields_first, fields_last, send_gram = pl.pallas_call(
        functools.partial(edges_of_sides_kernel, members),
        out_shape=[half, half, shape(n_lat * n_lon, LANES)],
        in_specs=[VMEM] * 8,
        out_specs=[VMEM] * 3,
        scratch_shapes=scratch([KINDS, KINDS], 2 * groups, 1),
        compiler_params=PARAMS,
        cost_estimate=cost(0.01),
        name="edges_of_sides",
    )(centre_first, centre_last, halo_a, halo_b, corners, facts, hist_e, strip_base)

    got = lax.all_to_all(send_gram, ("lon", "lat"), 0, 0, tiled=True)

    return pl.pallas_call(
        functools.partial(finish_kernel, members, float(3 * total_rows * total_cols)),
        out_shape=[shape(*perturbations.shape), shape(members, members)],
        in_specs=[VMEM] * 3,
        out_specs=[HBM, HBM],
        scratch_shapes=[
            pltpu.VMEM(perturbations.shape, f32),
            pltpu.VMEM((members, members), f32),
            pltpu.SemaphoreType.DMA((members + 1,)),
        ],
        compiler_params=PARAMS,
        name="finish",
    )(fields_first, fields_last, got)


def solution(mesh):
    return jax.shard_map(
        per_device,
        mesh=mesh,
        in_specs=(P(None, None, "lat", "lon"), P(None, "lat", "lon"), P("lat", "lon")),
        out_specs=(P(None, None, "lat", "lon"), P()),
        check_vma=False,
    )
```

```python
import functools
import math

import jax
import jax.numpy as jnp
from jax import lax
from jax.experimental import pallas as pl
from jax.experimental.pallas import tpu as pltpu
from jax.sharding import PartitionSpec as P

STEPS = 8
HALO = STEPS
TILE = 8
LANES = 128
FACTS = 40
STRIP = 3 * HALO
SLOTS = LANES // STRIP
MIX = 2 * STRIP + HALO
KINDS = 3
NCOEF = 18
SPARE = 2

advect_rate = 0.1
turn_rate = 0.5
gravity_rate = 0.2
diffuse_rate = 0.12

f32 = jnp.float32
VMEM = pl.BlockSpec(memory_space=pltpu.VMEM)
HBM = pl.BlockSpec(memory_space=pltpu.HBM)
PARAMS = pltpu.CompilerParams(vmem_limit_bytes=40 * 1024 * 1024)


def rotate(x, amount):
    amount = amount % LANES
    return x if amount == 0 else pltpu.roll(x, amount, axis=x.ndim - 1)


def lane_ids(rows=TILE):
    return lax.broadcasted_iota(jnp.int32, (rows, LANES), 1)


def dynamic_zero():
    return jnp.minimum(lax.axis_index("lat"), 0)


def is_inner():
    lat = lax.axis_index("lat")
    return jnp.where((lat > 0) & (lat < lax.axis_size("lat") - 1), 1, 0)


def is_north(last):
    toward_a = 1 - is_inner() if last else is_inner()
    return lax.rem(toward_a + lax.axis_index("lat"), 2) == 0


def is_even(axis):
    return lax.rem(lax.axis_index(axis), 2) == 0


def store_coefs(base, at, stride, facts, facts_at, coef, coef_at, tiles):
    half = 0.5 * advect_rate
    for t in tiles:
        m = facts[0, pl.ds(facts_at + TILE * t, TILE), :]
        turn = facts[1, pl.ds(facts_at + TILE * t, TILE), :]

        def three(v):
            return [base[pl.ds(at + v * stride + TILE * t + d, TILE), :] for d in range(3)]

        us, u, un = three(0)
        vs, v, vn = three(1)
        hs, h, hn = three(2)
        ue, ve, he = rotate(u, -1), rotate(v, -1), rotate(h, -1)
        uw, vw, hw = rotate(u, 1), rotate(v, 1), rotate(h, 1)
        centre = (1.0 - 4.0 * diffuse_rate) * m
        dif = diffuse_rate * m
        am = half * m
        values = [
            dif - am * u,
            dif + am * u,
            dif - am * v,
            dif + am * v,
            centre - am * (ue - uw),
            turn - am * (un - us),
            centre - am * (vn - vs),
            -turn - am * (ve - vw),
            (0.5 * gravity_rate) * m,
            dif - am * ue,
            dif + am * uw,
            dif - am * vn,
            dif + am * vs,
            -am * he,
            am * hw,
            -am * hn,
            am * hs,
            centre,
        ]
        for i, value in enumerate(values):
            coef[pl.ds(coef_at + i * FACTS + TILE * t, TILE), :] = value


def load_coefs(coef, at):
    return [coef[pl.ds(at + i * FACTS, TILE), :] for i in range(NCOEF)]


def step_tile(src, at, stride, coefs):
    (ae, aw, an, as_, cu, du, cv, dv, k1, he, hw, hn, hs, ue, uw, vn, vs, c0) = coefs

    def three(v):
        return [src[pl.ds(at + v * stride + d, TILE), :] for d in range(3)]

    u_s, u, u_n = three(0)
    v_s, v, v_n = three(1)
    h_s, h, h_n = three(2)
    u_e, v_e, h_e = rotate(u, -1), rotate(v, -1), rotate(h, -1)
    u_w, v_w, h_w = rotate(u, 1), rotate(v, 1), rotate(h, 1)
    new_u = (ae * u_e + aw * u_w) + (an * u_n + as_ * u_s) + (cu * u + du * v) + k1 * (h_w - h_e)
    new_v = (ae * v_e + aw * v_w) + (an * v_n + as_ * v_s) + (cv * v + dv * u) + k1 * (h_s - h_n)
    new_h = (he * h_e + hw * h_w) + (hn * h_n + hs * h_s) + (ue * u_e + uw * u_w) + (vn * v_n + vs * v_s) + c0 * h
    return new_u, new_v, new_h


PYRAMID = 24
FRONT = 8


def pyramid(refs, zero, work, hist):
    def keep(step, source, plane):
        start = zero + FRONT + plane * PYRAMID
        hist[0, step, plane] = source[pl.ds(start, TILE), :]
        hist[1, step, plane] = source[pl.ds(start + TILE - 2 * step, TILE), :]

    for step in range(1, STEPS):
        src, dst = refs[(step - 1) % 2], refs[step % 2]
        for t in range(-(-(16 - 2 * step) // TILE)):
            for coef, coef_at, triples in work:
                coefs = load_coefs(coef, coef_at + TILE * t + step - 1)
                for triple in triples:
                    at = FRONT + 3 * triple * PYRAMID + TILE * t
                    new = step_tile(src, zero + at, PYRAMID, coefs)
                    for v in range(3):
                        dst[pl.ds(zero + at + v * PYRAMID, TILE), :] = new[v]
        for _, _, triples in work:
            for triple in triples:
                for v in range(3):
                    keep(step, dst, 3 * triple + v)


def first_level(hist, plane, low, high):
    hist[0, 0, plane] = low
    hist[1, 0, plane] = high


def slot_range(s, shift):
    lanes = (lane_ids() + shift) % LANES
    return (lanes >= STRIP * s) & (lanes < STRIP * s + STRIP)


def in_strip():
    return lane_ids() % STRIP


def own_strips(rows_of, members):
    wests, easts = [], []
    for q in range(members // SLOTS):
        west = east = None
        for s in range(SLOTS):
            moved = rotate(rows_of(SLOTS * q + s), STRIP * s + HALO)
            west = moved if s == 0 else jnp.where(slot_range(s, 0), moved, west)
            east = moved if s == 0 else jnp.where(slot_range(s, HALO), moved, east)
        wests.append(west)
        easts.append(east)
    left = members % SLOTS
    mixed = None
    for s in range(2 * left):
        moved = rotate(rows_of(members - left + s % left), STRIP * s + (HALO if s < left else 2 * HALO))
        mixed = moved if s == 0 else jnp.where(slot_range(s, 0), moved, mixed)
    return wests + easts + [mixed]


def fill_strips(vectors, west_halo, east_halo, members):
    place = in_strip()
    full, left = members // SLOTS, members % SLOTS
    filled = []
    for q in range(full):
        filled.append(jnp.where(place < HALO, rotate(west_halo, -HALO * q), vectors[q]))
    inner = (place >= HALO) & (place < 2 * HALO)
    for q in range(full):
        filled.append(jnp.where(inner, rotate(east_halo, -HALO * q), vectors[full + q]))
    lanes = lane_ids()
    mixed = jnp.where((place < HALO) & (lanes < left * STRIP), rotate(west_halo, -HALO * full), vectors[-1])
    outer = (place >= 2 * HALO) & (lanes >= left * STRIP)
    return filled + [jnp.where(outer, rotate(east_halo, MIX - HALO * full), mixed)]


def base_strips(rows, west_halo, east_halo, members):
    q, left = members // SLOTS, members % SLOTS
    place = in_strip()
    lanes = lane_ids()
    west = east = mixed = None
    for s in range(SLOTS):
        moved = rotate(rows, STRIP * s + HALO)
        west = moved if s == 0 else jnp.where(slot_range(s, 0), moved, west)
        east = moved if s == 0 else jnp.where(slot_range(s, HALO), moved, east)
        if s < 2 * left:
            over = moved if s < left else rotate(rows, STRIP * s + 2 * HALO)
            mixed = over if s == 0 else jnp.where(slot_range(s, 0), over, mixed)
    near = [rotate(halo, -HALO * q) for halo in (west_halo, east_halo)]
    far = [rotate(halo, -HALO * q - STRIP * left) for halo in (west_halo, east_halo)]
    low = lanes < left * STRIP
    west = jnp.where(place < HALO, jnp.where(low, far[0], near[0]), west)
    inner = (place >= HALO) & (place < 2 * HALO)
    east = jnp.where(inner, jnp.where(lanes < left * STRIP + HALO, far[1], near[1]), east)
    mixed = jnp.where((place < HALO) & low, far[0], mixed)
    outer = (place >= 2 * HALO) & (lanes >= left * STRIP)
    return west, east, jnp.where(outer, rotate(east_halo, MIX - HALO * q - STRIP * left), mixed)


def strip_kinds(members):
    full = members // SLOTS
    return [0] * full + [1] * full + [2]


def load_kernel(members, pert, wind, height, own, main_a, msg_a, msg_b, sems):
    copies = [
        pltpu.make_async_copy(pert, own.at[pl.ds(0, members)], sems.at[0]),
        pltpu.make_async_copy(wind, own.at[members, pl.ds(0, 2)], sems.at[1]),
        pltpu.make_async_copy(height, own.at[members, 2], sems.at[2]),
    ]
    for copy in copies:
        copy.start()
    for copy in copies:
        copy.wait()
    low = pl.multiple_of(jnp.where(is_even("lat"), TILE, 0), TILE)
    for m in range(SPARE):
        main_a[members + 1 + m] = jnp.zeros((3, TILE, LANES), f32)
    for m in range(members + 1):
        for v in range(3):
            main_a[m, v] = own[m, v, pl.ds(low, TILE), :]
    lon_even = is_even("lon")
    lanes = lane_ids()
    for v in range(3):
        for t in range(2):
            rows = slice(TILE * t, TILE * t + TILE)
            to_e = to_w = None
            for q in range(3):
                for s in range(SLOTS):
                    low = STRIP * s + HALO * q
                    moved = rotate(own[min(SLOTS * q + s, members), v, rows, :], low + HALO)
                    if to_e is None:
                        to_e = to_w = moved
                    else:
                        to_e = jnp.where((lanes >= low) & (lanes < low + HALO), moved, to_e)
                        to_w = jnp.where((lanes >= low + HALO) & (lanes < low + 2 * HALO), moved, to_w)
            msg_a[v, rows, :] = jnp.where(lon_even, to_e, to_w)
            msg_b[v, rows, :] = jnp.where(lon_even, to_w, to_e)


def centre_kernel(members, total_rows, own, facts, hist, first, second, base, coef):
    zero = dynamic_zero()
    start = lax.axis_index("lat") * 16 - HALO + 1
    for t in range(FACTS // TILE):
        glob = start + TILE * t + lax.broadcasted_iota(jnp.int32, (TILE, LANES), 0)
        inside = ((glob >= 0) & (glob < total_rows)).astype(f32)
        rows = slice(TILE * t, TILE * t + TILE)
        facts[0, rows, :] = inside
        facts[1, rows, :] = turn_rate * inside * jnp.sin(math.pi * ((glob.astype(f32) + 0.5) / total_rows - 0.5))
    for m in range(members + 1):
        for v in range(3):
            low, high = own[m, v, 0:TILE, :], own[m, v, TILE:16, :]
            plane = 3 * m + v
            if m < members:
                ref, at = first, FRONT + plane * PYRAMID
                first_level(hist, plane, low, high)
            else:
                ref, at = base, FRONT + v * PYRAMID
            ref[at : at + TILE, :] = low
            ref[at + TILE : at + 16, :] = high
    store_coefs(base, zero + FRONT, PYRAMID, facts, HALO, coef, zero, range(2))
    pyramid([first, second], zero, [(coef, zero, list(range(members)))], hist)


def meet_kernel(members, own, got_b, got_a, send_b, west, east, corners):
    lon_even = is_even("lon")
    low = pl.multiple_of(jnp.where(is_even("lat"), 0, TILE), TILE)
    for v in range(3):
        for t in range(2):
            rows = slice(TILE * t, TILE * t + TILE)
            west[v, rows, :] = jnp.where(lon_even, got_b[v, rows, :], got_a[v, rows, :])
            east[v, rows, :] = jnp.where(lon_even, got_a[v, rows, :], got_b[v, rows, :])
    for m in range(members + 1):
        for v in range(3):
            send_b[m, v] = own[m, v, pl.ds(low, TILE), :]
    for v in range(3):
        for side, halo in enumerate((west, east)):
            send_b[members + 1 + side, v] = halo[v, pl.ds(low, TILE), :]
            corners[side, v] = halo[v, pl.ds(pl.multiple_of(TILE - low, TILE), TILE), :]


def edges_kernel(members, own, west, east, facts, hist, strip_base, first, second, base, coef):
    zero = dynamic_zero()
    kinds = strip_kinds(members)
    for v in range(3):
        for t in range(2):
            rows = slice(TILE * t, TILE * t + TILE)
            halos = west[v, rows, :], east[v, rows, :]
            strips = fill_strips(own_strips(lambda m: own[m, v, rows, :], members), *halos, members)
            for g, strip in enumerate(strips):
                at = FRONT + (3 * g + v) * PYRAMID + TILE * t
                first[at : at + TILE, :] = strip
                hist[t, 0, 3 * g + v] = strip
            for kind, strip in enumerate(base_strips(own[members, v, rows, :], *halos, members)):
                at = FRONT + (3 * kind + v) * PYRAMID + TILE * t
                base[at : at + TILE, :] = strip
                strip_base[kind, v, rows, :] = strip
    work = []
    for kind in range(KINDS):
        coef_at = zero + kind * NCOEF * FACTS
        store_coefs(base, zero + FRONT + 3 * kind * PYRAMID, PYRAMID, facts, HALO, coef, coef_at, range(2))
        work.append((coef, coef_at, [g for g in range(len(kinds)) if kinds[g] == kind]))
    pyramid([first, second], zero, work, hist)


WEDGE = 16
BASE = 40


class Side:
    def __init__(self, last):
        north = is_north(last)
        self.north = north
        self.index = jnp.where(north, 0, 1)
        self.wedge_at = jnp.where(north, 0, TILE)
        self.lean_at = jnp.where(north, TILE, 0)
        self.read_at = jnp.where(north, 0, TILE - 2)
        self.own_at = jnp.where(north, 2 * TILE, 1)
        self.halo_at = jnp.where(north, TILE, 2 * TILE + 1)
        self.facts_at = jnp.where(north, 0, 2 * TILE - 1)
        self.zero = dynamic_zero()

    def wedge(self, v):
        return pl.ds(self.wedge_at + v * WEDGE, TILE)

    def put_base(self, base, plane, own, halo):
        for t in range(2):
            base[pl.ds(self.own_at + plane * BASE + TILE * t, TILE), :] = own(t)
        base[pl.ds(self.halo_at + plane * BASE, TILE), :] = halo

    def coefs(self, base, kind, facts, coef):
        coef_at = self.zero + kind * NCOEF * FACTS
        at = self.zero + TILE + 3 * kind * BASE
        store_coefs(base, at, BASE, facts, self.facts_at, coef, coef_at, range(2))
        return coef_at


def prepare_centre(side, members, own, halo, facts, base, coef, first):
    for m in range(members):
        for v in range(3):
            first[m][side.wedge(v), :] = halo(m, v)
    for v in range(3):
        side.put_base(base, v, lambda t: own[members, v, TILE * t : TILE * t + TILE, :], halo(members, v))
    return [(coef, side.coefs(base, 0, facts, coef), list(range(members)))]


def prepare_edges(side, members, halo, corner, facts, strip_base, base, coef, first, ready=None):
    kinds = strip_kinds(members)
    for v in range(3):
        west, east = corner(v)
        if ready is None:
            own = own_strips(lambda m: halo(m, v), members)
        else:
            own = [ready[v, g] for g in range(len(kinds))]
        strips = fill_strips(own, west, east, members)
        for g, strip in enumerate(strips):
            first[members + g][side.wedge(v), :] = strip
        for kind, strip in enumerate(base_strips(halo(members, v), west, east, members)):
            side.put_base(base, 3 * kind + v, lambda t: strip_base[kind, v, TILE * t : TILE * t + TILE, :], strip)
    return [
        (coef, side.coefs(base, kind, facts, coef), [members + g for g in range(len(kinds)) if kinds[g] == kind])
        for kind in range(KINDS)
    ]


def run_wedges(members, jobs):
    def lean(job, step):
        side, work, hist_c, hist_e, *refs = job
        for _, _, part in work:
            for triple in part:
                hist, plane = (hist_c, 3 * triple) if triple < members else (hist_e, 3 * (triple - members))
                for v in range(3):
                    refs[step % 2][triple][pl.ds(side.lean_at + v * WEDGE, TILE), :] = hist[side.index, step, plane + v]

    for job in jobs:
        lean(job, 0)
    for step in range(1, STEPS + 1):
        for job in jobs:
            side, work, _, _, *refs = job
            src, dst = refs[(step - 1) % 2], refs[step % 2]
            row = jnp.where(side.north, step - 1, STEPS - step)
            for ref, coef_at, part in work:
                coefs = load_coefs(ref, coef_at + row)
                for triple in part:
                    new = step_tile(src[triple], side.read_at, WEDGE, coefs)
                    for v in range(3):
                        dst[triple][side.wedge(v), :] = new[v]
            if step < STEPS:
                lean(job, step)


def merge(side, members, done, inner, fields):
    place = in_strip()
    lanes = lane_ids()
    edge = (lanes < HALO) | (lanes >= LANES - HALO)
    full = members // SLOTS
    for v in range(3):

        def strip(g):
            return done[members + g][side.wedge(v), :]

        for q in range(full + 1):
            west, east = (strip(q), strip(full + q)) if q < full else (strip(2 * full), rotate(strip(2 * full), -MIX))
            both = jnp.where((place >= HALO) & (place < 2 * HALO), west, east)
            for s in range(min(SLOTS, members - SLOTS * q)):
                m = SLOTS * q + s
                fields[m, v] = jnp.where(edge, rotate(both, -STRIP * s - HALO), inner(m, v))


def pair_sums(members, fields_1, fields_2, pairs):
    for i in range(members):
        for j in range(i, members):
            at = TILE * pair_place(i, j, members)
            products = [ref[i, v] * ref[j, v] for ref in (fields_1, fields_2) for v in range(3)]
            pairs[at : at + TILE, :] = sum(products[1:], products[0])
    sums = []
    for a in range(members + 1):
        for b in range(members // 2, TILE):
            at = TILE * (TILE * a + b)
            pairs[at : at + TILE, :] = jnp.zeros((TILE, LANES), f32)
        total = pairs[pl.ds(TILE * TILE * a, TILE, stride=TILE), :]
        for s in range(1, TILE):
            total = total + pairs[pl.ds(TILE * TILE * a + s, TILE, stride=TILE), :]
        sums.append(total)
    return sums


def centre_side(side, members, own, halo, facts, hist_c, centre, base, coef, wedges):
    first, second = wedges[:members], wedges[members:]
    work = prepare_centre(side, members, own, halo, facts, base, coef, first)
    run_wedges(members, [(side, work, hist_c, None, first, second)])
    for m in range(members):
        for v in range(3):
            centre[m, v] = first[m][side.wedge(v), :]


def first_rows(halo_a):
    inner = is_inner() == 1
    return lambda m, v: jnp.where(inner, halo_a[m, v], 0.0)


def last_rows(halo_a, halo_b):
    inner = is_inner() == 1
    return lambda m, v: jnp.where(inner, halo_b[m, v], halo_a[m, v])


def first_centre_kernel(members, own, halo_a, facts, hist_c, centre, ready, base, coef, *wedges):
    rows = first_rows(halo_a)
    for v in range(3):
        for g, strip in enumerate(own_strips(lambda m: rows(m, v), members)):
            ready[v, g] = strip
    centre_side(Side(False), members, own, first_rows(halo_a), facts, hist_c, centre, base, coef, wedges)


def last_centre_kernel(members, own, halo_a, halo_b, facts, hist_c, centre, base, coef, *wedges):
    centre_side(Side(True), members, own, last_rows(halo_a, halo_b), facts, hist_c, centre, base, coef, wedges)


def edges_of_sides_kernel(
    members, centre_1, ready, centre_2, halo_a, halo_b, corners, facts, hist_e, strip_base, fields_1, fields_2, result, *scratch
):
    inner = is_inner() == 1
    bases, coefs, pairs, wedges = scratch[0:2], scratch[2:4], scratch[4], scratch[5:]
    groups = len(wedges) // 4

    def corner_first(v):
        return tuple(jnp.where(inner, corners[i, v], 0.0) for i in range(2))

    def corner_last(v):
        return tuple(jnp.where(inner, halo_b[members + 1 + i, v], corners[i, v]) for i in range(2))

    jobs = []
    halos = (first_rows(halo_a), corner_first), (last_rows(halo_a, halo_b), corner_last)
    for n, (halo, corner) in enumerate(halos):
        side = Side(n == 1)
        part = wedges[2 * n * groups : 2 * (n + 1) * groups]
        first = {members + g: part[g] for g in range(groups)}
        second = {members + g: part[groups + g] for g in range(groups)}
        work = prepare_edges(side, members, halo, corner, facts, strip_base, bases[n], coefs[n], first, [ready, None][n])
        jobs.append((side, work, None, hist_e, first, second))
    run_wedges(members, jobs)
    for n, (centre, fields) in enumerate(((centre_1, fields_1), (centre_2, fields_2))):
        merge(jobs[n][0], members, jobs[n][4], lambda m, v: centre[m, v], fields)
    sums = pair_sums(members, fields_1, fields_2, pairs)
    lanes = lane_ids()
    packed = jnp.zeros((TILE, LANES), f32)
    for a, total in enumerate(sums):
        packed = jnp.where(lanes == a, jnp.sum(total, axis=1, keepdims=True), packed)
    packed = pltpu.roll(packed, 0, axis=1, stride=SPREAD, stride_axis=0)
    result[...] = jnp.broadcast_to(jnp.sum(packed, axis=0, keepdims=True), result.shape)


SPREAD = LANES // TILE


def pair_place(i, j, members):
    b = min(i, members - 1 - i)
    a = j - b if i == b else j + 1
    return TILE * a + b


def finish_kernel(members, count, fields_a, fields_b, got, out, factor_out, done, factor, sems):
    total = got[0:TILE, :]
    for r in range(TILE, got.shape[0], TILE):
        total = total + got[r : r + TILE, :]
    packed = jnp.sum(total, axis=0, keepdims=True) / count
    packed = jnp.broadcast_to(packed, (TILE, LANES))
    gram = {}
    for i in range(members):
        for j in range(i, members):
            place = pair_place(i, j, members)
            lane = SPREAD * (place % TILE) + place // TILE
            gram[i, j] = jnp.broadcast_to(packed[:, lane : lane + 1], (TILE, LANES))
    first_at = pl.multiple_of(jnp.where(is_north(False), 0, TILE), TILE)
    places = [first_at, pl.multiple_of(TILE - first_at, TILE)]
    x = [[[ref[m, v] for v in range(3)] for ref in (fields_a, fields_b)] for m in range(members)]
    lanes = lane_ids()
    copies = []
    for k in range(members):
        scale = lax.rsqrt(gram[k, k])
        for half in range(2):
            for v in range(3):
                x[k][half][v] = x[k][half][v] * scale
                done[k, v, pl.ds(places[half], TILE), :] = x[k][half][v]
        copy = pltpu.make_async_copy(done.at[k], out.at[k], sems.at[k])
        copy.start()
        copies.append(copy)
        row = jnp.zeros((TILE, LANES), f32)
        for i in range(k, members):
            gram[k, i] = gram[k, i] * scale
            row = jnp.where(lanes == i, gram[k, i], row)
        factor[k : k + 1, :] = row[0:1, :members]
        for i in range(k + 1, members):
            for j in range(i, members):
                gram[i, j] = gram[i, j] - gram[k, i] * gram[k, j]
            for half in range(2):
                for v in range(3):
                    x[i][half][v] = x[i][half][v] - gram[k, i] * x[k][half][v]
    copy = pltpu.make_async_copy(factor, factor_out, sems.at[members])
    copy.start()
    for copy in copies + [copy]:
        copy.wait()


def swap(block, axis, count, even_up, periodic):
    pairs = []
    for i in range(count):
        other = i + 1 if (i % 2 == 0) == even_up else i - 1
        if periodic:
            other %= count
        if 0 <= other < count:
            pairs.append((i, other))
    return lax.ppermute(block, axis, pairs)


def shape(*dims):
    return jax.ShapeDtypeStruct(dims, f32)


def cost(micros):
    return pl.CostEstimate(flops=0, bytes_accessed=int(micros * 3.6e6), transcendentals=0)


def per_device(perturbations, base_wind, base_height):
    members, _, rows, cols = perturbations.shape
    n_lat, n_lon = lax.axis_size("lat"), lax.axis_size("lon")
    total_rows, total_cols = rows * n_lat, cols * n_lon
    groups = len(strip_kinds(members))
    planes_c, planes_e = 3 * members, 3 * groups

    own, main_a, msg_a, msg_b = pl.pallas_call(
        functools.partial(load_kernel, members),
        out_shape=[
            shape(members + 1, 3, rows, LANES),
            shape(members + 1 + SPARE, 3, TILE, LANES),
            shape(3, rows, LANES),
            shape(3, rows, LANES),
        ],
        in_specs=[HBM] * 3,
        out_specs=[VMEM] * 4,
        scratch_shapes=[pltpu.SemaphoreType.DMA((3,))],
        compiler_params=PARAMS,
        name="load",
    )(*(pltpu.with_memory_space_constraint(x, pltpu.HBM) for x in (perturbations, base_wind, base_height)))
    halo_a = swap(main_a, "lat", n_lat, True, False)
    got_b = swap(msg_b, "lon", n_lon, False, True)
    got_a = swap(msg_a, "lon", n_lon, True, True)

    facts, hist_c = pl.pallas_call(
        functools.partial(centre_kernel, members, total_rows),
        out_shape=[shape(2, FACTS, LANES), shape(2, STEPS, planes_c, TILE, LANES)],
        in_specs=[VMEM],
        out_specs=[VMEM] * 2,
        scratch_shapes=[
            pltpu.VMEM((FRONT + planes_c * PYRAMID, LANES), f32),
            pltpu.VMEM((FRONT + planes_c * PYRAMID, LANES), f32),
            pltpu.VMEM((FRONT + 3 * PYRAMID, LANES), f32),
            pltpu.VMEM((NCOEF * FACTS, LANES), f32),
        ],
        compiler_params=PARAMS,
        cost_estimate=cost(20),
        name="centre",
    )(own)

    send_b, west, east, corners = pl.pallas_call(
        functools.partial(meet_kernel, members),
        out_shape=[
            shape(members + 3, 3, TILE, LANES),
            shape(3, rows, LANES),
            shape(3, rows, LANES),
            shape(2, 3, TILE, LANES),
        ],
        in_specs=[VMEM] * 3,
        out_specs=[VMEM] * 4,
        compiler_params=PARAMS,
        cost_estimate=cost(0.01),
        name="meet",
    )(own, got_b, got_a)
    halo_b = swap(send_b, "lat", n_lat, False, False)
    corners = swap(corners, "lat", n_lat, True, False)

    hist_e, strip_base = pl.pallas_call(
        functools.partial(edges_kernel, members),
        out_shape=[shape(2, STEPS, planes_e, TILE, LANES), shape(KINDS, 3, rows, LANES)],
        in_specs=[VMEM] * 4,
        out_specs=[VMEM] * 2,
        scratch_shapes=[
            pltpu.VMEM((FRONT + planes_e * PYRAMID, LANES), f32),
            pltpu.VMEM((FRONT + planes_e * PYRAMID, LANES), f32),
            pltpu.VMEM((FRONT + 3 * KINDS * PYRAMID, LANES), f32),
            pltpu.VMEM((KINDS * NCOEF * FACTS, LANES), f32),
        ],
        compiler_params=PARAMS,
        cost_estimate=cost(0.01),
        name="edges",
    )(own, west, east, facts)

    def scratch(bases, triples, with_pairs):
        shapes = [(3 * n * BASE, LANES) for n in bases] + [(n * NCOEF * FACTS, LANES) for n in bases]
        shapes += [(TILE * LANES, LANES)] * with_pairs + [(3 * WEDGE, LANES)] * (2 * triples)
        return [pltpu.VMEM(dims, f32) for dims in shapes]

    half = shape(members, 3, TILE, LANES)
    centre_first, ready = pl.pallas_call(
        functools.partial(first_centre_kernel, members),
        out_shape=[half, shape(3, groups, TILE, LANES)],
        in_specs=[VMEM] * 4,
        out_specs=[VMEM] * 2,
        scratch_shapes=scratch([1], members, 0),
        compiler_params=PARAMS,
        cost_estimate=cost(0.01),
        name="first_centre",
    )(own, halo_a, facts, hist_c)
    centre_last = pl.pallas_call(
        functools.partial(last_centre_kernel, members),
        out_shape=half,
        in_specs=[VMEM] * 5,
        out_specs=VMEM,
        scratch_shapes=scratch([1], members, 0),
        compiler_params=PARAMS,
        cost_estimate=cost(0.01),
        name="last_centre",
    )(own, halo_a, halo_b, facts, hist_c)
    fields_first, fields_last, send_gram = pl.pallas_call(
        functools.partial(edges_of_sides_kernel, members),
        out_shape=[half, half, shape(n_lat * n_lon, LANES)],
        in_specs=[VMEM] * 9,
        out_specs=[VMEM] * 3,
        scratch_shapes=scratch([KINDS, KINDS], 2 * groups, 1),
        compiler_params=PARAMS,
        cost_estimate=cost(0.01),
        name="edges_of_sides",
    )(centre_first, ready, centre_last, halo_a, halo_b, corners, facts, hist_e, strip_base)

    got = lax.all_to_all(send_gram, ("lon", "lat"), 0, 0, tiled=True)

    return pl.pallas_call(
        functools.partial(finish_kernel, members, float(3 * total_rows * total_cols)),
        out_shape=[shape(*perturbations.shape), shape(members, members)],
        in_specs=[VMEM] * 3,
        out_specs=[HBM, HBM],
        scratch_shapes=[
            pltpu.VMEM(perturbations.shape, f32),
            pltpu.VMEM((members, members), f32),
            pltpu.SemaphoreType.DMA((members + 1,)),
        ],
        compiler_params=PARAMS,
        name="finish",
    )(fields_first, fields_last, got)


def solution(mesh):
    return jax.shard_map(
        per_device,
        mesh=mesh,
        in_specs=(P(None, None, "lat", "lon"), P(None, "lat", "lon"), P("lat", "lon")),
        out_specs=(P(None, None, "lat", "lon"), P()),
        check_vma=False,
    )
```

```python
import functools
import math

import jax
import jax.numpy as jnp
from jax import lax
from jax.experimental import pallas as pl
from jax.experimental.pallas import tpu as pltpu
from jax.sharding import PartitionSpec as P

STEPS = 8
HALO = STEPS
TILE = 8
LANES = 128
FACTS = 40
STRIP = 3 * HALO
SLOTS = LANES // STRIP
MIX = 2 * STRIP + HALO
KINDS = 3
NCOEF = 18
SPARE = 2

advect_rate = 0.1
turn_rate = 0.5
gravity_rate = 0.2
diffuse_rate = 0.12

f32 = jnp.float32
VMEM = pl.BlockSpec(memory_space=pltpu.VMEM)
HBM = pl.BlockSpec(memory_space=pltpu.HBM)
PARAMS = pltpu.CompilerParams(vmem_limit_bytes=40 * 1024 * 1024)


def rotate(x, amount):
    amount = amount % LANES
    return x if amount == 0 else pltpu.roll(x, amount, axis=x.ndim - 1)


def lane_ids(rows=TILE):
    return lax.broadcasted_iota(jnp.int32, (rows, LANES), 1)


def dynamic_zero():
    return jnp.minimum(lax.axis_index("lat"), 0)


def is_inner():
    lat = lax.axis_index("lat")
    return jnp.where((lat > 0) & (lat < lax.axis_size("lat") - 1), 1, 0)


def is_north(last):
    toward_a = 1 - is_inner() if last else is_inner()
    return lax.rem(toward_a + lax.axis_index("lat"), 2) == 0


def is_even(axis):
    return lax.rem(lax.axis_index(axis), 2) == 0


def store_coefs(base, at, stride, facts, facts_at, coef, coef_at, tiles):
    half = 0.5 * advect_rate
    for t in tiles:
        m = facts[0, pl.ds(facts_at + TILE * t, TILE), :]
        turn = facts[1, pl.ds(facts_at + TILE * t, TILE), :]

        def three(v):
            return [base[pl.ds(at + v * stride + TILE * t + d, TILE), :] for d in range(3)]

        us, u, un = three(0)
        vs, v, vn = three(1)
        hs, h, hn = three(2)
        ue, ve, he = rotate(u, -1), rotate(v, -1), rotate(h, -1)
        uw, vw, hw = rotate(u, 1), rotate(v, 1), rotate(h, 1)
        centre = (1.0 - 4.0 * diffuse_rate) * m
        dif = diffuse_rate * m
        am = half * m
        values = [
            dif - am * u,
            dif + am * u,
            dif - am * v,
            dif + am * v,
            centre - am * (ue - uw),
            turn - am * (un - us),
            centre - am * (vn - vs),
            -turn - am * (ve - vw),
            (0.5 * gravity_rate) * m,
            dif - am * ue,
            dif + am * uw,
            dif - am * vn,
            dif + am * vs,
            -am * he,
            am * hw,
            -am * hn,
            am * hs,
            centre,
        ]
        for i, value in enumerate(values):
            coef[pl.ds(coef_at + i * FACTS + TILE * t, TILE), :] = value


def load_coefs(coef, at):
    return [coef[pl.ds(at + i * FACTS, TILE), :] for i in range(NCOEF)]


def step_tile(src, at, stride, coefs):
    (ae, aw, an, as_, cu, du, cv, dv, k1, he, hw, hn, hs, ue, uw, vn, vs, c0) = coefs

    def three(v):
        return [src[pl.ds(at + v * stride + d, TILE), :] for d in range(3)]

    u_s, u, u_n = three(0)
    v_s, v, v_n = three(1)
    h_s, h, h_n = three(2)
    u_e, v_e, h_e = rotate(u, -1), rotate(v, -1), rotate(h, -1)
    u_w, v_w, h_w = rotate(u, 1), rotate(v, 1), rotate(h, 1)
    new_u = (ae * u_e + aw * u_w) + (an * u_n + as_ * u_s) + (cu * u + du * v) + k1 * (h_w - h_e)
    new_v = (ae * v_e + aw * v_w) + (an * v_n + as_ * v_s) + (cv * v + dv * u) + k1 * (h_s - h_n)
    new_h = (he * h_e + hw * h_w) + (hn * h_n + hs * h_s) + (ue * u_e + uw * u_w) + (vn * v_n + vs * v_s) + c0 * h
    return new_u, new_v, new_h


PYRAMID = 24
FRONT = 8


def pyramid(refs, zero, work, hist):
    def keep(step, source, plane):
        start = zero + FRONT + plane * PYRAMID
        hist[0, step, plane] = source[pl.ds(start, TILE), :]
        hist[1, step, plane] = source[pl.ds(start + TILE - 2 * step, TILE), :]

    for step in range(1, STEPS):
        src, dst = refs[(step - 1) % 2], refs[step % 2]
        for t in range(-(-(16 - 2 * step) // TILE)):
            for coef, coef_at, triples in work:
                coefs = load_coefs(coef, coef_at + TILE * t + step - 1)
                for triple in triples:
                    at = FRONT + 3 * triple * PYRAMID + TILE * t
                    new = step_tile(src, zero + at, PYRAMID, coefs)
                    for v in range(3):
                        dst[pl.ds(zero + at + v * PYRAMID, TILE), :] = new[v]
        for _, _, triples in work:
            for triple in triples:
                for v in range(3):
                    keep(step, dst, 3 * triple + v)


def first_level(hist, plane, low, high):
    hist[0, 0, plane] = low
    hist[1, 0, plane] = high


def slot_range(s, shift):
    lanes = (lane_ids() + shift) % LANES
    return (lanes >= STRIP * s) & (lanes < STRIP * s + STRIP)


def in_strip():
    return lane_ids() % STRIP


def own_strips(rows_of, members):
    wests, easts = [], []
    for q in range(members // SLOTS):
        west = east = None
        for s in range(SLOTS):
            moved = rotate(rows_of(SLOTS * q + s), STRIP * s + HALO)
            west = moved if s == 0 else jnp.where(slot_range(s, 0), moved, west)
            east = moved if s == 0 else jnp.where(slot_range(s, HALO), moved, east)
        wests.append(west)
        easts.append(east)
    left = members % SLOTS
    mixed = None
    for s in range(2 * left):
        moved = rotate(rows_of(members - left + s % left), STRIP * s + (HALO if s < left else 2 * HALO))
        mixed = moved if s == 0 else jnp.where(slot_range(s, 0), moved, mixed)
    return wests + easts + [mixed]


def fill_strips(vectors, west_halo, east_halo, members):
    place = in_strip()
    full, left = members // SLOTS, members % SLOTS
    filled = []
    for q in range(full):
        filled.append(jnp.where(place < HALO, rotate(west_halo, -HALO * q), vectors[q]))
    inner = (place >= HALO) & (place < 2 * HALO)
    for q in range(full):
        filled.append(jnp.where(inner, rotate(east_halo, -HALO * q), vectors[full + q]))
    lanes = lane_ids()
    mixed = jnp.where((place < HALO) & (lanes < left * STRIP), rotate(west_halo, -HALO * full), vectors[-1])
    outer = (place >= 2 * HALO) & (lanes >= left * STRIP)
    return filled + [jnp.where(outer, rotate(east_halo, MIX - HALO * full), mixed)]


def base_own_strips(rows, members):
    left = members % SLOTS
    west = east = mixed = None
    for s in range(SLOTS):
        moved = rotate(rows, STRIP * s + HALO)
        west = moved if s == 0 else jnp.where(slot_range(s, 0), moved, west)
        east = moved if s == 0 else jnp.where(slot_range(s, HALO), moved, east)
        if s < 2 * left:
            over = moved if s < left else rotate(rows, STRIP * s + 2 * HALO)
            mixed = over if s == 0 else jnp.where(slot_range(s, 0), over, mixed)
    return west, east, mixed


def base_strips(own, west_halo, east_halo, members):
    west, east, mixed = own
    q, left = members // SLOTS, members % SLOTS
    place = in_strip()
    lanes = lane_ids()
    near = [rotate(halo, -HALO * q) for halo in (west_halo, east_halo)]
    far = [rotate(halo, -HALO * q - STRIP * left) for halo in (west_halo, east_halo)]
    low = lanes < left * STRIP
    west = jnp.where(place < HALO, jnp.where(low, far[0], near[0]), west)
    inner = (place >= HALO) & (place < 2 * HALO)
    east = jnp.where(inner, jnp.where(lanes < left * STRIP + HALO, far[1], near[1]), east)
    mixed = jnp.where((place < HALO) & low, far[0], mixed)
    outer = (place >= 2 * HALO) & (lanes >= left * STRIP)
    return west, east, jnp.where(outer, rotate(east_halo, MIX - HALO * q - STRIP * left), mixed)


def strip_kinds(members):
    full = members // SLOTS
    return [0] * full + [1] * full + [2]


def load_kernel(members, pert, wind, height, own, main_a, msg_a, msg_b, sems):
    copies = [
        pltpu.make_async_copy(pert, own.at[pl.ds(0, members)], sems.at[0]),
        pltpu.make_async_copy(wind, own.at[members, pl.ds(0, 2)], sems.at[1]),
        pltpu.make_async_copy(height, own.at[members, 2], sems.at[2]),
    ]
    for copy in copies:
        copy.start()
    for copy in copies:
        copy.wait()
    low = pl.multiple_of(jnp.where(is_even("lat"), TILE, 0), TILE)
    for m in range(SPARE):
        main_a[members + 1 + m] = jnp.zeros((3, TILE, LANES), f32)
    for m in range(members + 1):
        for v in range(3):
            main_a[m, v] = own[m, v, pl.ds(low, TILE), :]
    lon_even = is_even("lon")
    lanes = lane_ids()
    for v in range(3):
        for t in range(2):
            rows = slice(TILE * t, TILE * t + TILE)
            to_e = to_w = None
            for q in range(3):
                for s in range(SLOTS):
                    low = STRIP * s + HALO * q
                    moved = rotate(own[min(SLOTS * q + s, members), v, rows, :], low + HALO)
                    if to_e is None:
                        to_e = to_w = moved
                    else:
                        to_e = jnp.where((lanes >= low) & (lanes < low + HALO), moved, to_e)
                        to_w = jnp.where((lanes >= low + HALO) & (lanes < low + 2 * HALO), moved, to_w)
            msg_a[v, rows, :] = jnp.where(lon_even, to_e, to_w)
            msg_b[v, rows, :] = jnp.where(lon_even, to_w, to_e)


def centre_kernel(members, total_rows, own, facts, hist, first, second, base, coef):
    zero = dynamic_zero()
    start = lax.axis_index("lat") * 16 - HALO + 1
    for t in range(FACTS // TILE):
        glob = start + TILE * t + lax.broadcasted_iota(jnp.int32, (TILE, LANES), 0)
        inside = ((glob >= 0) & (glob < total_rows)).astype(f32)
        rows = slice(TILE * t, TILE * t + TILE)
        facts[0, rows, :] = inside
        facts[1, rows, :] = turn_rate * inside * jnp.sin(math.pi * ((glob.astype(f32) + 0.5) / total_rows - 0.5))
    for m in range(members + 1):
        for v in range(3):
            low, high = own[m, v, 0:TILE, :], own[m, v, TILE:16, :]
            plane = 3 * m + v
            if m < members:
                ref, at = first, FRONT + plane * PYRAMID
                first_level(hist, plane, low, high)
            else:
                ref, at = base, FRONT + v * PYRAMID
            ref[at : at + TILE, :] = low
            ref[at + TILE : at + 16, :] = high
    store_coefs(base, zero + FRONT, PYRAMID, facts, HALO, coef, zero, range(2))
    pyramid([first, second], zero, [(coef, zero, list(range(members)))], hist)


def meet_kernel(members, own, got_b, got_a, send_b, west, east, corners):
    lon_even = is_even("lon")
    low = pl.multiple_of(jnp.where(is_even("lat"), 0, TILE), TILE)
    for v in range(3):
        for t in range(2):
            rows = slice(TILE * t, TILE * t + TILE)
            west[v, rows, :] = jnp.where(lon_even, got_b[v, rows, :], got_a[v, rows, :])
            east[v, rows, :] = jnp.where(lon_even, got_a[v, rows, :], got_b[v, rows, :])
    for m in range(members + 1):
        for v in range(3):
            send_b[m, v] = own[m, v, pl.ds(low, TILE), :]
    for v in range(3):
        for side, halo in enumerate((west, east)):
            send_b[members + 1 + side, v] = halo[v, pl.ds(low, TILE), :]
            corners[side, v] = halo[v, pl.ds(pl.multiple_of(TILE - low, TILE), TILE), :]


def edges_kernel(members, own, west, east, facts, hist, strip_base, first, second, base, coef):
    zero = dynamic_zero()
    kinds = strip_kinds(members)
    for v in range(3):
        for t in range(2):
            rows = slice(TILE * t, TILE * t + TILE)
            halos = west[v, rows, :], east[v, rows, :]
            strips = fill_strips(own_strips(lambda m: own[m, v, rows, :], members), *halos, members)
            for g, strip in enumerate(strips):
                at = FRONT + (3 * g + v) * PYRAMID + TILE * t
                first[at : at + TILE, :] = strip
                hist[t, 0, 3 * g + v] = strip
            for kind, strip in enumerate(base_strips(base_own_strips(own[members, v, rows, :], members), *halos, members)):
                at = FRONT + (3 * kind + v) * PYRAMID + TILE * t
                base[at : at + TILE, :] = strip
                strip_base[kind, v, rows, :] = strip
    work = []
    for kind in range(KINDS):
        coef_at = zero + kind * NCOEF * FACTS
        store_coefs(base, zero + FRONT + 3 * kind * PYRAMID, PYRAMID, facts, HALO, coef, coef_at, range(2))
        work.append((coef, coef_at, [g for g in range(len(kinds)) if kinds[g] == kind]))
    pyramid([first, second], zero, work, hist)


WEDGE = 16
BASE = 40


class Side:
    def __init__(self, last):
        north = is_north(last)
        self.north = north
        self.index = jnp.where(north, 0, 1)
        self.wedge_at = jnp.where(north, 0, TILE)
        self.lean_at = jnp.where(north, TILE, 0)
        self.read_at = jnp.where(north, 0, TILE - 2)
        self.own_at = jnp.where(north, 2 * TILE, 1)
        self.halo_at = jnp.where(north, TILE, 2 * TILE + 1)
        self.facts_at = jnp.where(north, 0, 2 * TILE - 1)
        self.zero = dynamic_zero()

    def wedge(self, v):
        return pl.ds(self.wedge_at + v * WEDGE, TILE)

    def put_base(self, base, plane, own, halo):
        for t in range(2):
            base[pl.ds(self.own_at + plane * BASE + TILE * t, TILE), :] = own(t)
        base[pl.ds(self.halo_at + plane * BASE, TILE), :] = halo

    def coefs(self, base, kind, facts, coef):
        coef_at = self.zero + kind * NCOEF * FACTS
        at = self.zero + TILE + 3 * kind * BASE
        store_coefs(base, at, BASE, facts, self.facts_at, coef, coef_at, range(2))
        return coef_at


def prepare_centre(side, members, own, halo, facts, base, coef, first):
    for m in range(members):
        for v in range(3):
            first[m][side.wedge(v), :] = halo(m, v)
    for v in range(3):
        side.put_base(base, v, lambda t: own[members, v, TILE * t : TILE * t + TILE, :], halo(members, v))
    return [(coef, side.coefs(base, 0, facts, coef), list(range(members)))]


def prepare_edges(side, members, halo, corner, facts, strip_base, base, coef, first, ready=None):
    kinds = strip_kinds(members)
    for v in range(3):
        west, east = corner(v)
        if ready is None:
            own = own_strips(lambda m: halo(m, v), members)
            own_base = base_own_strips(halo(members, v), members)
        else:
            own = [ready[v, g] for g in range(len(kinds))]
            own_base = [ready[v, len(kinds) + kind] for kind in range(KINDS)]
        strips = fill_strips(own, west, east, members)
        for g, strip in enumerate(strips):
            first[members + g][side.wedge(v), :] = strip
        for kind, strip in enumerate(base_strips(own_base, west, east, members)):
            side.put_base(base, 3 * kind + v, lambda t: strip_base[kind, v, TILE * t : TILE * t + TILE, :], strip)
    return [
        (coef, side.coefs(base, kind, facts, coef), [members + g for g in range(len(kinds)) if kinds[g] == kind])
        for kind in range(KINDS)
    ]


def run_wedges(members, jobs):
    def lean(job, step):
        side, work, hist_c, hist_e, *refs = job
        for _, _, part in work:
            for triple in part:
                hist, plane = (hist_c, 3 * triple) if triple < members else (hist_e, 3 * (triple - members))
                for v in range(3):
                    refs[step % 2][triple][pl.ds(side.lean_at + v * WEDGE, TILE), :] = hist[side.index, step, plane + v]

    for job in jobs:
        lean(job, 0)
    for step in range(1, STEPS + 1):
        for job in jobs:
            side, work, _, _, *refs = job
            src, dst = refs[(step - 1) % 2], refs[step % 2]
            row = jnp.where(side.north, step - 1, STEPS - step)
            for ref, coef_at, part in work:
                coefs = load_coefs(ref, coef_at + row)
                for triple in part:
                    new = step_tile(src[triple], side.read_at, WEDGE, coefs)
                    for v in range(3):
                        dst[triple][side.wedge(v), :] = new[v]
            if step < STEPS:
                lean(job, step)


def merge(side, members, done, inner, fields):
    place = in_strip()
    lanes = lane_ids()
    edge = (lanes < HALO) | (lanes >= LANES - HALO)
    full = members // SLOTS
    for v in range(3):

        def strip(g):
            return done[members + g][side.wedge(v), :]

        for q in range(full + 1):
            west, east = (strip(q), strip(full + q)) if q < full else (strip(2 * full), rotate(strip(2 * full), -MIX))
            both = jnp.where((place >= HALO) & (place < 2 * HALO), west, east)
            for s in range(min(SLOTS, members - SLOTS * q)):
                m = SLOTS * q + s
                fields[m, v] = jnp.where(edge, rotate(both, -STRIP * s - HALO), inner(m, v))


def pair_sums(members, fields_1, fields_2, pairs):
    for i in range(members):
        for j in range(i, members):
            at = TILE * pair_place(i, j, members)
            products = [ref[i, v] * ref[j, v] for ref in (fields_1, fields_2) for v in range(3)]
            pairs[at : at + TILE, :] = sum(products[1:], products[0])
    sums = []
    for a in range(members + 1):
        for b in range(members // 2, TILE):
            at = TILE * (TILE * a + b)
            pairs[at : at + TILE, :] = jnp.zeros((TILE, LANES), f32)
        total = pairs[pl.ds(TILE * TILE * a, TILE, stride=TILE), :]
        for s in range(1, TILE):
            total = total + pairs[pl.ds(TILE * TILE * a + s, TILE, stride=TILE), :]
        sums.append(total)
    return sums


def centre_side(side, members, own, halo, facts, hist_c, centre, base, coef, wedges):
    first, second = wedges[:members], wedges[members:]
    work = prepare_centre(side, members, own, halo, facts, base, coef, first)
    run_wedges(members, [(side, work, hist_c, None, first, second)])
    for m in range(members):
        for v in range(3):
            centre[m, v] = first[m][side.wedge(v), :]


def first_rows(halo_a):
    inner = is_inner() == 1
    return lambda m, v: jnp.where(inner, halo_a[m, v], 0.0)


def last_rows(halo_a, halo_b):
    inner = is_inner() == 1
    return lambda m, v: jnp.where(inner, halo_b[m, v], halo_a[m, v])


def first_centre_kernel(members, own, halo_a, facts, hist_c, centre, ready, base, coef, *wedges):
    rows = first_rows(halo_a)
    for v in range(3):
        strips = own_strips(lambda m: rows(m, v), members) + list(base_own_strips(rows(members, v), members))
        for g, strip in enumerate(strips):
            ready[v, g] = strip
    centre_side(Side(False), members, own, first_rows(halo_a), facts, hist_c, centre, base, coef, wedges)


def last_centre_kernel(members, own, halo_a, halo_b, facts, hist_c, centre, base, coef, *wedges):
    centre_side(Side(True), members, own, last_rows(halo_a, halo_b), facts, hist_c, centre, base, coef, wedges)


def edges_of_sides_kernel(
    members, centre_1, ready, centre_2, halo_a, halo_b, corners, facts, hist_e, strip_base, fields_1, fields_2, result, *scratch
):
    inner = is_inner() == 1
    bases, coefs, pairs, wedges = scratch[0:2], scratch[2:4], scratch[4], scratch[5:]
    groups = len(wedges) // 4

    def corner_first(v):
        return tuple(jnp.where(inner, corners[i, v], 0.0) for i in range(2))

    def corner_last(v):
        return tuple(jnp.where(inner, halo_b[members + 1 + i, v], corners[i, v]) for i in range(2))

    jobs = []
    halos = (first_rows(halo_a), corner_first), (last_rows(halo_a, halo_b), corner_last)
    for n, (halo, corner) in enumerate(halos):
        side = Side(n == 1)
        part = wedges[2 * n * groups : 2 * (n + 1) * groups]
        first = {members + g: part[g] for g in range(groups)}
        second = {members + g: part[groups + g] for g in range(groups)}
        work = prepare_edges(side, members, halo, corner, facts, strip_base, bases[n], coefs[n], first, [ready, None][n])
        jobs.append((side, work, None, hist_e, first, second))
    run_wedges(members, jobs)
    for n, (centre, fields) in enumerate(((centre_1, fields_1), (centre_2, fields_2))):
        merge(jobs[n][0], members, jobs[n][4], lambda m, v: centre[m, v], fields)
    sums = pair_sums(members, fields_1, fields_2, pairs)
    lanes = lane_ids()
    packed = jnp.zeros((TILE, LANES), f32)
    for a, total in enumerate(sums):
        packed = jnp.where(lanes == a, jnp.sum(total, axis=1, keepdims=True), packed)
    packed = pltpu.roll(packed, 0, axis=1, stride=SPREAD, stride_axis=0)
    result[...] = jnp.broadcast_to(jnp.sum(packed, axis=0, keepdims=True), result.shape)


SPREAD = LANES // TILE


def pair_place(i, j, members):
    b = min(i, members - 1 - i)
    a = j - b if i == b else j + 1
    return TILE * a + b


def finish_kernel(members, count, fields_a, fields_b, got, out, factor_out, done, factor, sems):
    total = got[0:TILE, :]
    for r in range(TILE, got.shape[0], TILE):
        total = total + got[r : r + TILE, :]
    packed = jnp.sum(total, axis=0, keepdims=True) / count
    packed = jnp.broadcast_to(packed, (TILE, LANES))
    gram = {}
    for i in range(members):
        for j in range(i, members):
            place = pair_place(i, j, members)
            lane = SPREAD * (place % TILE) + place // TILE
            gram[i, j] = jnp.broadcast_to(packed[:, lane : lane + 1], (TILE, LANES))
    first_at = pl.multiple_of(jnp.where(is_north(False), 0, TILE), TILE)
    places = [first_at, pl.multiple_of(TILE - first_at, TILE)]
    x = [[[ref[m, v] for v in range(3)] for ref in (fields_a, fields_b)] for m in range(members)]
    lanes = lane_ids()
    copies = []
    for k in range(members):
        scale = lax.rsqrt(gram[k, k])
        for half in range(2):
            for v in range(3):
                x[k][half][v] = x[k][half][v] * scale
                done[k, v, pl.ds(places[half], TILE), :] = x[k][half][v]
        copy = pltpu.make_async_copy(done.at[k], out.at[k], sems.at[k])
        copy.start()
        copies.append(copy)
        row = jnp.zeros((TILE, LANES), f32)
        for i in range(k, members):
            gram[k, i] = gram[k, i] * scale
            row = jnp.where(lanes == i, gram[k, i], row)
        factor[k : k + 1, :] = row[0:1, :members]
        for i in range(k + 1, members):
            for j in range(i, members):
                gram[i, j] = gram[i, j] - gram[k, i] * gram[k, j]
            for half in range(2):
                for v in range(3):
                    x[i][half][v] = x[i][half][v] - gram[k, i] * x[k][half][v]
    copy = pltpu.make_async_copy(factor, factor_out, sems.at[members])
    copy.start()
    for copy in copies + [copy]:
        copy.wait()


def swap(block, axis, count, even_up, periodic):
    pairs = []
    for i in range(count):
        other = i + 1 if (i % 2 == 0) == even_up else i - 1
        if periodic:
            other %= count
        if 0 <= other < count:
            pairs.append((i, other))
    return lax.ppermute(block, axis, pairs)


def shape(*dims):
    return jax.ShapeDtypeStruct(dims, f32)


def cost(micros):
    return pl.CostEstimate(flops=0, bytes_accessed=int(micros * 3.6e6), transcendentals=0)


def per_device(perturbations, base_wind, base_height):
    members, _, rows, cols = perturbations.shape
    n_lat, n_lon = lax.axis_size("lat"), lax.axis_size("lon")
    total_rows, total_cols = rows * n_lat, cols * n_lon
    groups = len(strip_kinds(members))
    planes_c, planes_e = 3 * members, 3 * groups

    own, main_a, msg_a, msg_b = pl.pallas_call(
        functools.partial(load_kernel, members),
        out_shape=[
            shape(members + 1, 3, rows, LANES),
            shape(members + 1 + SPARE, 3, TILE, LANES),
            shape(3, rows, LANES),
            shape(3, rows, LANES),
        ],
        in_specs=[HBM] * 3,
        out_specs=[VMEM] * 4,
        scratch_shapes=[pltpu.SemaphoreType.DMA((3,))],
        compiler_params=PARAMS,
        name="load",
    )(*(pltpu.with_memory_space_constraint(x, pltpu.HBM) for x in (perturbations, base_wind, base_height)))
    halo_a = swap(main_a, "lat", n_lat, True, False)
    got_b = swap(msg_b, "lon", n_lon, False, True)
    got_a = swap(msg_a, "lon", n_lon, True, True)

    facts, hist_c = pl.pallas_call(
        functools.partial(centre_kernel, members, total_rows),
        out_shape=[shape(2, FACTS, LANES), shape(2, STEPS, planes_c, TILE, LANES)],
        in_specs=[VMEM],
        out_specs=[VMEM] * 2,
        scratch_shapes=[
            pltpu.VMEM((FRONT + planes_c * PYRAMID, LANES), f32),
            pltpu.VMEM((FRONT + planes_c * PYRAMID, LANES), f32),
            pltpu.VMEM((FRONT + 3 * PYRAMID, LANES), f32),
            pltpu.VMEM((NCOEF * FACTS, LANES), f32),
        ],
        compiler_params=PARAMS,
        cost_estimate=cost(20),
        name="centre",
    )(own)

    send_b, west, east, corners = pl.pallas_call(
        functools.partial(meet_kernel, members),
        out_shape=[
            shape(members + 3, 3, TILE, LANES),
            shape(3, rows, LANES),
            shape(3, rows, LANES),
            shape(2, 3, TILE, LANES),
        ],
        in_specs=[VMEM] * 3,
        out_specs=[VMEM] * 4,
        compiler_params=PARAMS,
        cost_estimate=cost(0.01),
        name="meet",
    )(own, got_b, got_a)
    halo_b = swap(send_b, "lat", n_lat, False, False)
    corners = swap(corners, "lat", n_lat, True, False)

    hist_e, strip_base = pl.pallas_call(
        functools.partial(edges_kernel, members),
        out_shape=[shape(2, STEPS, planes_e, TILE, LANES), shape(KINDS, 3, rows, LANES)],
        in_specs=[VMEM] * 4,
        out_specs=[VMEM] * 2,
        scratch_shapes=[
            pltpu.VMEM((FRONT + planes_e * PYRAMID, LANES), f32),
            pltpu.VMEM((FRONT + planes_e * PYRAMID, LANES), f32),
            pltpu.VMEM((FRONT + 3 * KINDS * PYRAMID, LANES), f32),
            pltpu.VMEM((KINDS * NCOEF * FACTS, LANES), f32),
        ],
        compiler_params=PARAMS,
        cost_estimate=cost(0.01),
        name="edges",
    )(own, west, east, facts)

    def scratch(bases, triples, with_pairs):
        shapes = [(3 * n * BASE, LANES) for n in bases] + [(n * NCOEF * FACTS, LANES) for n in bases]
        shapes += [(TILE * LANES, LANES)] * with_pairs + [(3 * WEDGE, LANES)] * (2 * triples)
        return [pltpu.VMEM(dims, f32) for dims in shapes]

    half = shape(members, 3, TILE, LANES)
    centre_first, ready = pl.pallas_call(
        functools.partial(first_centre_kernel, members),
        out_shape=[half, shape(3, groups + KINDS, TILE, LANES)],
        in_specs=[VMEM] * 4,
        out_specs=[VMEM] * 2,
        scratch_shapes=scratch([1], members, 0),
        compiler_params=PARAMS,
        cost_estimate=cost(0.01),
        name="first_centre",
    )(own, halo_a, facts, hist_c)
    centre_last = pl.pallas_call(
        functools.partial(last_centre_kernel, members),
        out_shape=half,
        in_specs=[VMEM] * 5,
        out_specs=VMEM,
        scratch_shapes=scratch([1], members, 0),
        compiler_params=PARAMS,
        cost_estimate=cost(0.01),
        name="last_centre",
    )(own, halo_a, halo_b, facts, hist_c)
    fields_first, fields_last, send_gram = pl.pallas_call(
        functools.partial(edges_of_sides_kernel, members),
        out_shape=[half, half, shape(n_lat * n_lon, LANES)],
        in_specs=[VMEM] * 9,
        out_specs=[VMEM] * 3,
        scratch_shapes=scratch([KINDS, KINDS], 2 * groups, 1),
        compiler_params=PARAMS,
        cost_estimate=cost(0.01),
        name="edges_of_sides",
    )(centre_first, ready, centre_last, halo_a, halo_b, corners, facts, hist_e, strip_base)

    got = lax.all_to_all(send_gram, ("lon", "lat"), 0, 0, tiled=True)

    return pl.pallas_call(
        functools.partial(finish_kernel, members, float(3 * total_rows * total_cols)),
        out_shape=[shape(*perturbations.shape), shape(members, members)],
        in_specs=[VMEM] * 3,
        out_specs=[HBM, HBM],
        scratch_shapes=[
            pltpu.VMEM(perturbations.shape, f32),
            pltpu.VMEM((members, members), f32),
            pltpu.SemaphoreType.DMA((members + 1,)),
        ],
        compiler_params=PARAMS,
        name="finish",
    )(fields_first, fields_last, got)


def solution(mesh):
    return jax.shard_map(
        per_device,
        mesh=mesh,
        in_specs=(P(None, None, "lat", "lon"), P(None, "lat", "lon"), P("lat", "lon")),
        out_specs=(P(None, None, "lat", "lon"), P()),
        check_vma=False,
    )
```
